512 devices in a mesh: seq: 128 (over z_lo, y, x), ch: 4 (over z_hi, core).
Axes of the slice: x: 4, y: 4, z: 16 (z_hi: 2, z_lo: 8; z = z_hi * 8 + z_lo), core: 2. Of those that a mesh axis runs over, the one named last changes fastest.
Arguments:
- queries: bfloat16 [512, 16384], P('ch', 'seq'), may hold values from -6 to 6
- key_inputs: bfloat16 [512, 16384], P('ch', 'seq'), may hold values from -6 to 6
- value_inputs: bfloat16 [512, 16384], P('ch', 'seq'), may hold values from -6 to 6
- skip_gain: float32 [512], P('ch'), may hold values from -4 to 4
- residue: float32 [32, 16], P('ch'), may hold values from -4 to 4
- timescale: float32 [32, 16], P('ch'), may hold values from 20 to 32768
- cotangent: bfloat16 [512, 16384], P('ch', 'seq'), may hold values from -6 to 6
Outputs:
- output: bfloat16 [512, 16384], P('ch', 'seq')
- grad_queries: bfloat16 [512, 16384], P('ch', 'seq')
- grad_keys: bfloat16 [512, 16384], P('ch', 'seq')
- grad_values: bfloat16 [512, 16384], P('ch', 'seq')
- grad_skip: float32 [512], P('ch')
- grad_residue: float32 [32, 16], replicated
- grad_timescale: float32 [32, 16], replicated
The draws below stay inside these ranges and needn't reach their ends.
All inputs are finite; a program needn't handle non-finite values.
Results may differ from the reference program's by a relative error of at most 0.0023.
Values sent between devices are 32-bit elements; how exact they have to be, the bound alone decides.
No kernel may reach another device: no remote copies, remote signals or barrier semaphores. Data moves between devices by JAX's collectives and lax.ppermute only.
A program may use at most 64 MiB of HBM per device.

```python
import math
import jax
import jax.numpy as jnp
from jax import lax

CHANNELS = 512
GROUP_CH = 16
ORDER = 16
TOKENS = 16384
GROUPS = 32


def draw_timescale(key, part):
    key = jax.random.fold_in(key, 11)
    select_key, spread_key = jax.random.split(key)
    selector = jax.random.uniform(select_key, (GROUPS, ORDER), jnp.float32)
    fraction = jax.random.uniform(spread_key, (GROUPS, ORDER), jnp.float32)
    fast_share, middle_share = (0.35, 0.15)
    log_short = math.log(20.0)
    log_mid = math.log(50.0)
    log_half = math.log(TOKENS * 0.5)
    log_long = math.log(TOKENS * 2.0)
    log_fast = log_short + fraction * (log_mid - log_short)
    log_middle = log_mid + fraction * (log_half - log_mid)
    log_slow = log_half + fraction * (log_long - log_half)
    chosen = jnp.where(selector < fast_share, log_fast, jnp.where(selector < fast_share + middle_share, log_middle, log_slow))
    return jnp.clip(jnp.exp(chosen), 20.0, TOKENS * 2.0)


def block_scale(own_key, extent, cuts, low, top_value):
    factor_of, own = 1.0, jax.random.fold_in(own_key, 6)
    for position, shards_of in cuts:
        steps = jnp.exp(jax.random.uniform(jax.random.fold_in(own, position), (shards_of,), jnp.float32, low / len(cuts), top_value / len(cuts)))
        factor_of = factor_of * jnp.repeat(steps, extent[position] // shards_of).reshape([-1 if axis == position else 1 for axis in range(len(extent))])
    return factor_of


def gaussian(stream_key, dims, width, reach, shards=(), held_as=jnp.bfloat16):
    array = width * jax.random.normal(stream_key, dims, jnp.float32)
    if shards:
        array = array * block_scale(stream_key, dims, shards, -0.22, 0.18)
    return jnp.clip(array, -reach, reach).astype(held_as)


def setup_inputs(seed: int = 0) -> dict:
    streams_of = jax.random.split(jax.random.key(seed), 8)
    queries = gaussian(streams_of[0], (CHANNELS, TOKENS), 1.0, 6.0, ((0, 4), (1, 128)))
    key_inputs = gaussian(streams_of[1], (CHANNELS, TOKENS), 1.0, 6.0, ((0, 4), (1, 128)))
    value_inputs = gaussian(streams_of[2], (CHANNELS, TOKENS), 1.0, 6.0, ((0, 4), (1, 128)))
    skip_gain = gaussian(streams_of[3], (CHANNELS,), 1.0, 4.0, ((0, 4),), jnp.float32)
    residue = gaussian(streams_of[4], (GROUPS, ORDER), 1.0, 4.0, ((0, 4),), jnp.float32)
    timescale = draw_timescale(jax.random.fold_in(streams_of[7], 71), 0)
    cotangent = gaussian(streams_of[6], (CHANNELS, TOKENS), 1.0, 6.0, ((0, 4), (1, 128)))
    return {"queries": queries, "key_inputs": key_inputs, "value_inputs": value_inputs, "skip_gain": skip_gain, "residue": residue, "timescale": timescale, "cotangent": cotangent}


def filter_rows(residue, timescale, positions):
    decay_rate = 1.0 / timescale
    amplitude = residue * jnp.sqrt(2.0 * decay_rate) / math.sqrt(residue.shape[-1])
    return lax.optimization_barrier(jnp.sum(amplitude[:, :, None] * jnp.exp(-positions[None, None, :] * decay_rate[:, :, None]), axis=1))

def reference(queries, key_inputs, value_inputs, skip_gain, residue, timescale, cotangent):
    positions = jnp.arange(TOKENS, dtype=jnp.int32).astype(jnp.float32)
    query_float = queries.astype(jnp.float32)
    key_float = key_inputs.astype(jnp.float32)
    value_float = value_inputs.astype(jnp.float32)
    cot_float = cotangent.astype(jnp.float32)
    product = query_float * key_float
    kernel = filter_rows(residue, timescale, positions)
    padded = 2 * TOKENS
    spec_product = jnp.fft.rfft(product, n=padded, axis=-1)
    spec_kernel = jnp.fft.rfft(kernel, n=padded, axis=-1)
    kernel_rows = jnp.repeat(spec_kernel, GROUP_CH, axis=0)
    convolved = jnp.fft.irfft(spec_product * kernel_rows, n=padded, axis=-1)[:, :TOKENS]
    mixed = convolved + skip_gain[:, None] * product
    output = (value_float * mixed).astype(jnp.bfloat16)
    grad_values = (cot_float * mixed).astype(jnp.bfloat16)
    grad_mixed = cot_float * value_float
    spec_grad = jnp.fft.rfft(grad_mixed, n=padded, axis=-1)
    grad_product = jnp.fft.irfft(jnp.conj(kernel_rows) * spec_grad, n=padded, axis=-1)[:, :TOKENS]
    grad_product = grad_product + skip_gain[:, None] * grad_mixed
    grad_queries = (grad_product * key_float).astype(jnp.bfloat16)
    grad_keys = (grad_product * query_float).astype(jnp.bfloat16)
    pair_spec = jnp.conj(spec_product) * spec_grad
    kernel_spec = lax.optimization_barrier(jnp.sum(pair_spec.reshape(GROUPS, GROUP_CH, pair_spec.shape[-1]), axis=1))
    grad_kernel = jnp.fft.irfft(kernel_spec, n=padded, axis=-1)[:, :TOKENS]
    grad_skip = lax.optimization_barrier(jnp.sum(grad_mixed * product, axis=1)) / math.sqrt(TOKENS)
    _, pullback = jax.vjp(lambda res_arg, time_arg: filter_rows(res_arg, time_arg, positions), residue, timescale)
    part_residue, part_time = pullback(grad_kernel)
    grad_scale = 1.0 / math.sqrt(TOKENS * GROUP_CH)
    return (output, grad_queries, grad_keys, grad_values, grad_skip, part_residue * grad_scale, part_time * timescale * grad_scale)
```

```python
import math

import jax
import jax.numpy as jnp
from jax import lax
from jax.experimental import pallas as pl
from jax.experimental.pallas import tpu as pltpu
from jax.sharding import Mesh, PartitionSpec as P

F32 = jnp.float32
HI = lax.Precision.HIGHEST
L = 128
CH = 128
G = 8
R = 16
M = 16
SUM_ROW = 4 * R
ROWS = SUM_ROW + 8
NP = 16
NZ = 8


def dot(a, b, ca=1, cb=0):
    return lax.dot_general(a, b, (((ca,), (cb,)), ((), ())), precision=HI, preferred_element_type=F32)


def iota(shape, axis):
    return lax.broadcasted_iota(jnp.int32, shape, axis)


def ones_where(cond):
    return jnp.where(cond, jnp.float32(1), jnp.float32(0))


def by_mode_and_channel(table):
    pick = ones_where(iota((G, CH), 1) // M == iota((G, CH), 0))
    return dot(table, pick, 0, 0)


def by_group_mode(table):
    pick = ones_where(iota((G * R, G), 0) // R == iota((G * R, G), 1))
    rows = dot(pick, table)
    rows = jnp.where(iota((G * R, R), 0) % R == iota((G * R, R), 1), rows, 0.0)
    return dot(rows, jnp.ones((R, L), F32))


def same_group():
    return iota((128, 128), 0) // M == iota((128, 128), 1) // M


def fold_states(full):
    own = jnp.where(same_group(), full, 0.0)
    return jnp.sum(own.reshape(G, R, CH), axis=0)


def spread_states(state):
    return jnp.where(same_group(), jnp.concatenate([state] * G, axis=0), 0.0)


def group_sums(h0, h1, skip_terms=None):
    pick = ones_where(iota((G, CH), 1) // M == iota((G, CH), 0))
    rows = jnp.concatenate([h0, h1, jnp.zeros((CH - 2 * R, CH), F32)], axis=0)
    return dot(pick, rows, 1, 1)


def local_kernel(q_ref, k_ref, v_ref, ct_ref, tau_ref, msg_ref):
    product = q_ref[...].astype(F32) * k_ref[...].astype(F32)
    grad_mixed = ct_ref[...].astype(F32) * v_ref[...].astype(F32)
    rate = by_group_mode(1.0 / tau_ref[...])
    lane = iota((128, 128), 1)
    row = iota((128, 128), 0)
    step = lane.astype(F32)
    decay = jnp.exp(-step * rate)
    left = jnp.float32(L) - step
    decay_end = jnp.exp(-left * rate)
    fwd = dot(jnp.concatenate([decay_end, left * decay_end], axis=0), product, 1, 1)
    bwd = dot(jnp.concatenate([decay, step * decay], axis=0), grad_mixed, 1, 1)
    flipped = dot(product, ones_where(lane + row == L - 1))
    inside = lane + row >= L - 1
    lags = []
    for g in range(G):
        c = slice(g * M, (g + 1) * M)
        outer = jnp.where(inside, dot(flipped[c], grad_mixed[c], 0, 0), 0.0)
        aligned = pltpu.roll(outer, 1, 1, stride=1, stride_axis=0)
        lags.append(jnp.sum(aligned, axis=0, keepdims=True))
    lags = jnp.concatenate(lags, axis=0)
    lags = jnp.concatenate([lags, lags * iota((G, L), 1).astype(F32)], axis=0)
    modal = dot(lags, decay, 1, 1)
    modal = jnp.where(iota((2 * G, G * R), 0) % G == iota((2 * G, G * R), 1) // R, modal, 0.0)
    sums = dot(modal[:G], ones_where(row % R == lane)) + dot(modal[G:], ones_where(row % R == lane - R))
    skip_col = jnp.sum(grad_mixed * product, axis=1, keepdims=True)
    skip_at = jnp.where(row % M == lane - 2 * R, skip_col, 0.0)
    pick = ones_where(iota((G, CH), 1) // M == iota((G, CH), 0))
    sums = sums + dot(pick, skip_at)
    message = jnp.concatenate(
        [fold_states(fwd[:128]), fold_states(bwd[:128]), fold_states(fwd[128:]), fold_states(bwd[128:]), sums], axis=0
    )
    for i in range(NP):
        msg_ref[i] = message


def conv_kernel(q_ref, k_ref, v_ref, ct_ref, tau_ref, res_ref, skip_ref, fwd_ref, bwd_ref, head_ref, tail_ref):
    product = q_ref[...].astype(F32) * k_ref[...].astype(F32)
    grad_mixed = ct_ref[...].astype(F32) * v_ref[...].astype(F32)
    inv = 1.0 / tau_ref[...]
    rate = by_group_mode(inv)
    gain = by_group_mode(res_ref[...] * jnp.sqrt(2.0 * inv) * (1.0 / math.sqrt(R)))
    lane = iota((128, 128), 1)
    row = iota((128, 128), 0)
    step = lane.astype(F32)
    head = gain * jnp.exp(-step * rate)
    head_ref[...] = head
    tail_ref[...] = gain * jnp.exp(-(jnp.float32(L) - step) * rate)
    taps = jnp.sum(head.reshape(G, R, L), axis=1)
    skip = jnp.sum(jnp.where(lane == row, skip_ref[...], 0.0), axis=1, keepdims=True)
    for g in range(G):
        c = slice(g * M, (g + 1) * M)
        table = pltpu.roll(jnp.broadcast_to(taps[g : g + 1], (L, L)), 0, 1, stride=1, stride_axis=0)
        table = jnp.where(lane >= row, table, 0.0)
        fwd_ref[c] = dot(product[c], table) + skip[c] * product[c]
        bwd_ref[c] = dot(grad_mixed[c], table, 1, 1) + skip[c] * grad_mixed[c]


def scan_states(msg_ref, count, rate, span, me):
    decay = jnp.exp(-jnp.float32(span) * rate)
    zero = jnp.zeros((R, CH), F32)
    part = lambda i, k: msg_ref[i, k * R : (k + 1) * R]
    f, f1, h0, h1, own_f = zero, zero, zero, zero, zero
    sums = jnp.zeros((G, 128), F32)
    for i in range(count):
        own_f = jnp.where(me == i, f, own_f)
        h0 = h0 + f * part(i, 1)
        h1 = h1 + f * part(i, 3) + f1 * part(i, 1)
        f1 = decay * (f1 + jnp.float32(span) * f) + part(i, 2)
        f = decay * f + part(i, 0)
        sums = sums + msg_ref[i, SUM_ROW : SUM_ROW + G]
    b, b1, own_b = zero, zero, zero
    for i in reversed(range(count)):
        own_b = jnp.where(me == i, b, own_b)
        b1 = decay * (b1 + jnp.float32(span) * b) + part(i, 3)
        b = decay * b + part(i, 1)
    return own_f, own_b, f, b, f1, b1, sums + group_sums(h0, h1)


def plane_index():
    return lax.axis_index("y") * 4 + lax.axis_index("x")


def plane_kernel(msg_ref, tau_ref, out_ref, carry_ref):
    rate = by_mode_and_channel(1.0 / tau_ref[...])
    own_f, own_b, f, b, f1, b1, sums = scan_states(msg_ref, NP, rate, L, plane_index())
    carry_ref[:R] = own_f
    carry_ref[R:] = own_b
    message = jnp.concatenate([f, b, f1, b1, sums], axis=0)
    for i in range(NZ):
        out_ref[i] = message


def final_kernel(msg_ref, tau_ref, res_ref, plane_ref, carry_ref, param_ref, skip_ref):
    inv = 1.0 / tau_ref[...]
    rate = by_mode_and_channel(inv)
    me = plane_index().astype(F32)
    own_f, own_b, _, _, _, _, sums = scan_states(msg_ref, NZ, rate, L * NP, lax.axis_index("z"))
    carry_ref[:R] = plane_ref[:R] + jnp.exp(-(L * me) * rate) * own_f
    carry_ref[R:] = plane_ref[R:] + jnp.exp(-(L * (NP - 1 - me)) * rate) * own_b
    scale = 1.0 / math.sqrt(L * NP * NZ * M)
    h0, h1 = sums[:, :R], sums[:, R : 2 * R]
    root = jnp.sqrt(2.0 * inv) * (1.0 / math.sqrt(R))
    param_ref[:, :R] = h0 * root * scale
    param_ref[:, R : 2 * R] = res_ref[...] * root * (h1 * inv - 0.5 * h0) * scale
    param_ref[:, 2 * R :] = jnp.zeros((G, 128 - 2 * R), F32)
    lane = iota((128, 128), 1)
    row = iota((128, 128), 0)
    spread = dot(sums, ones_where(row - 2 * R == lane % M) * ones_where(row >= 2 * R) * ones_where(row < 3 * R))
    spread = jnp.where(iota((G, CH), 1) // M == iota((G, CH), 0), spread, 0.0)
    skip_ref[...] = jnp.sum(spread, axis=0, keepdims=True) * (1.0 / math.sqrt(L * NP * NZ))


def output_kernel(
    q_ref, k_ref, v_ref, ct_ref, fwd_ref, bwd_ref, head_ref, tail_ref, carry_ref, out_ref, gq_ref, gk_ref, gv_ref
):
    mixed = fwd_ref[...] + dot(spread_states(carry_ref[:R]), head_ref[...], 0, 0)
    grad_product = bwd_ref[...] + dot(spread_states(carry_ref[R:]), tail_ref[...], 0, 0)
    out_ref[...] = (v_ref[...].astype(F32) * mixed).astype(jnp.bfloat16)
    gv_ref[...] = (ct_ref[...].astype(F32) * mixed).astype(jnp.bfloat16)
    gq_ref[...] = (grad_product * k_ref[...].astype(F32)).astype(jnp.bfloat16)
    gk_ref[...] = (grad_product * q_ref[...].astype(F32)).astype(jnp.bfloat16)


def shape(*dims, dtype=F32):
    return jax.ShapeDtypeStruct(dims, dtype)


def call(kernel, outs, flops, name):
    return pl.pallas_call(
        kernel,
        out_shape=outs,
        name=name,
        cost_estimate=pl.CostEstimate(flops=flops, bytes_accessed=500_000, transcendentals=0),
        compiler_params=pltpu.CompilerParams(vmem_limit_bytes=32 * 1024 * 1024),
    )


def per_device(queries, key_inputs, value_inputs, skip_gain, residue, timescale, cotangent):
    arrays = (queries, key_inputs, value_inputs, cotangent)
    message = call(local_kernel, shape(NP, ROWS, 128), 10**8, "local_states")(*arrays, timescale)
    plane_states = lax.all_to_all(message, ("y", "x"), 0, 0)
    tables = call(conv_kernel, (shape(128, 128),) * 4, 10**8, "local_conv")(
        *arrays, timescale, residue, skip_gain.reshape(1, CH)
    )
    totals, plane_carry = call(plane_kernel, (shape(NZ, ROWS, 128), shape(2 * R, CH)), 10**7, "plane_scan")(
        plane_states, timescale
    )
    z_states = lax.all_to_all(totals, "z", 0, 0)
    carry, params, grad_skip = call(
        final_kernel, (shape(2 * R, CH), shape(G, 128), shape(1, CH)), 10**7, "z_scan"
    )(z_states, timescale, residue, plane_carry)
    swap = [(0, 1), (1, 0)]
    other = lax.ppermute(params, "zh", swap)
    outs = call(output_kernel, (shape(CH, L, dtype=jnp.bfloat16),) * 4, 10**8, "outputs")(
        *arrays, *tables, carry
    )
    flip = lax.axis_index("zh") == 1
    pair = jnp.stack([jnp.where(flip, other, params), jnp.where(flip, params, other)])
    other_pair = lax.ppermute(pair, "core", swap)
    odd = lax.axis_index("core") == 1
    whole = jnp.stack([jnp.where(odd, other_pair, pair), jnp.where(odd, pair, other_pair)], axis=1)
    whole = whole.reshape(4 * G, 128)
    output, grad_queries, grad_keys, grad_values = outs
    return (
        output,
        grad_queries,
        grad_keys,
        grad_values,
        grad_skip.reshape(CH),
        whole[:, :R],
        whole[:, R : 2 * R],
    )


def solution(mesh):
    grid = Mesh(mesh.devices.reshape(NZ, 4, 4, 2, 2), ("z", "y", "x", "zh", "core"))
    seq = ("z", "y", "x")
    ch = ("zh", "core")
    return jax.shard_map(
        per_device,
        mesh=grid,
        in_specs=(P(ch, seq), P(ch, seq), P(ch, seq), P(ch), P(ch, None), P(ch, None), P(ch, seq)),
        out_specs=(P(ch, seq), P(ch, seq), P(ch, seq), P(ch, seq), P(ch), P(), P()),
        check_vma=False,
    )
```

```python
import math

import jax
import jax.numpy as jnp
from jax import lax
from jax.experimental import pallas as pl
from jax.experimental.pallas import tpu as pltpu
from jax.sharding import Mesh, PartitionSpec as P

F32 = jnp.float32
HI = lax.Precision.HIGHEST
L = 128
CH = 128
G = 8
R = 16
M = 16
MOMENT_ROW = 2 * R
SUM_ROW = MOMENT_ROW + R // 2
ROWS = SUM_ROW + G
NP = 16
NZ = 8
SHARE = CH // 4
Z_ROWS = 2 * R + G
PEERS = 16


def dot(a, b, ca=1, cb=0):
    return lax.dot_general(a, b, (((ca,), (cb,)), ((), ())), precision=HI, preferred_element_type=F32)


def iota(shape, axis):
    return lax.broadcasted_iota(jnp.int32, shape, axis)


def ones_where(cond):
    return jnp.where(cond, jnp.float32(1), jnp.float32(0))


def by_mode_and_channel(table):
    pick = ones_where(iota((G, CH), 1) // M == iota((G, CH), 0))
    return dot(table, pick, 0, 0)


def by_group_mode(table):
    pick = ones_where(iota((G * R, G), 0) // R == iota((G * R, G), 1))
    rows = dot(pick, table)
    rows = jnp.where(iota((G * R, R), 0) % R == iota((G * R, R), 1), rows, 0.0)
    return dot(rows, jnp.ones((R, L), F32))


def same_group():
    return iota((128, 128), 0) // M == iota((128, 128), 1) // M


def fold_states(full):
    own = jnp.where(same_group(), full, 0.0)
    return jnp.sum(own.reshape(G, R, CH), axis=0)


def spread_states(state):
    return jnp.where(same_group(), jnp.concatenate([state] * G, axis=0), 0.0)


def group_sums(h0, h1):
    pick = ones_where(iota((G, CH), 1) // M == iota((G, CH), 0))
    rows = jnp.concatenate([h0, h1, jnp.zeros((CH - 2 * R, CH), F32)], axis=0)
    return dot(pick, rows, 1, 1)


def fetch(pairs, sems):
    copies = [pltpu.make_async_copy(src, dst, sems.at[i]) for i, (src, dst) in enumerate(pairs)]
    for copy in copies:
        copy.start()
    for copy in copies:
        copy.wait()


def local_kernel(
    q_hbm, k_hbm, v_hbm, ct_hbm, tau_hbm, res_hbm, msg_ref, table_ref, q_ref, k_ref, v_ref, ct_ref, tau_ref, res_ref, sems
):
    fetch(
        (
            (tau_hbm, tau_ref),
            (q_hbm, q_ref),
            (k_hbm, k_ref),
            (v_hbm, v_ref),
            (ct_hbm, ct_ref),
            (res_hbm, res_ref),
        ),
        sems,
    )
    table_ref[0] = tau_ref[...]
    table_ref[1] = res_ref[...]
    product = q_ref[...].astype(F32) * k_ref[...].astype(F32)
    grad_mixed = ct_ref[...].astype(F32) * v_ref[...].astype(F32)
    rate = by_group_mode(1.0 / tau_ref[...])
    lane = iota((128, 128), 1)
    row = iota((128, 128), 0)
    step = lane.astype(F32)
    decay = jnp.exp(-step * rate)
    left = jnp.float32(L) - step
    decay_end = jnp.exp(-left * rate)
    fwd = dot(jnp.concatenate([decay_end, left * decay_end], axis=0), product, 1, 1)
    bwd = dot(jnp.concatenate([decay, step * decay], axis=0), grad_mixed, 1, 1)
    flipped = dot(product, ones_where(lane + row == L - 1))
    inside = lane + row >= L - 1
    lags = []
    for g in range(G):
        c = slice(g * M, (g + 1) * M)
        outer = jnp.where(inside, dot(flipped[c], grad_mixed[c], 0, 0), 0.0)
        aligned = pltpu.roll(outer, 1, 1, stride=1, stride_axis=0)
        lags.append(jnp.sum(aligned, axis=0, keepdims=True))
    lags = jnp.concatenate(lags, axis=0)
    lags = jnp.concatenate([lags, lags * iota((G, L), 1).astype(F32)], axis=0)
    modal = dot(lags, decay, 1, 1)
    modal = jnp.where(iota((2 * G, G * R), 0) % G == iota((2 * G, G * R), 1) // R, modal, 0.0)
    sums = dot(modal[:G], ones_where(row % R == lane)) + dot(modal[G:], ones_where(row % R == lane - R))
    skip_col = jnp.sum(grad_mixed * product, axis=1, keepdims=True)
    skip_at = jnp.where(row % M == lane - 2 * R, skip_col, 0.0)
    pick = ones_where(iota((G, CH), 1) // M == iota((G, CH), 0))
    sums = sums + dot(pick, skip_at)
    states = jnp.concatenate([fold_states(fwd[:128]), fold_states(bwd[:128])], axis=0)
    moments = (fold_states(fwd[128:]), fold_states(bwd[128:]))
    quarters = (moments[0][:8], moments[0][8:], moments[1][:8], moments[1][8:])
    for y in range(4):
        packed = jnp.zeros((8, CH), F32)
        for k, quarter in enumerate(quarters):
            packed = jnp.where(lane[:8] // SHARE == k, pltpu.roll(quarter, (k - y) % 4 * SHARE, 1), packed)
        for x in range(4):
            msg_ref[4 * y + x, :MOMENT_ROW] = states
            msg_ref[4 * y + x, MOMENT_ROW:SUM_ROW] = packed
            msg_ref[4 * y + x, SUM_ROW:] = sums


def conv_kernel(
    q_hbm, k_hbm, v_hbm, ct_hbm, skip_hbm, table_ref, fwd_ref, bwd_ref, head_ref, tail_ref, q_ref, k_ref, v_ref, ct_ref, skip_ref, sems
):
    fetch(((q_hbm, q_ref), (k_hbm, k_ref), (v_hbm, v_ref), (ct_hbm, ct_ref), (skip_hbm, skip_ref)), sems)
    product = q_ref[...].astype(F32) * k_ref[...].astype(F32)
    grad_mixed = ct_ref[...].astype(F32) * v_ref[...].astype(F32)
    inv = 1.0 / table_ref[0]
    rate = by_group_mode(inv)
    gain = by_group_mode(table_ref[1] * jnp.sqrt(2.0 * inv) * (1.0 / math.sqrt(R)))
    lane = iota((128, 128), 1)
    row = iota((128, 128), 0)
    step = lane.astype(F32)
    head = gain * jnp.exp(-step * rate)
    head_ref[...] = head
    tail_ref[...] = gain * jnp.exp(-(jnp.float32(L) - step) * rate)
    taps = jnp.sum(head.reshape(G, R, L), axis=1)
    skip = jnp.sum(jnp.where(lane == row, skip_ref[...], 0.0), axis=1, keepdims=True)
    for g in range(G):
        c = slice(g * M, (g + 1) * M)
        table = pltpu.roll(jnp.broadcast_to(taps[g : g + 1], (L, L)), 0, 1, stride=1, stride_axis=0)
        table = jnp.where(lane >= row, table, 0.0)
        fwd_ref[c] = dot(product[c], table) + skip[c] * product[c]
        bwd_ref[c] = dot(grad_mixed[c], table, 1, 1) + skip[c] * grad_mixed[c]


def plane_index():
    return lax.axis_index("y") * 4 + lax.axis_index("x")


def plane_kernel(msg_ref, table_ref, out_ref, carry_ref):
    rate = by_mode_and_channel(1.0 / table_ref[0])
    me = plane_index()
    y = lax.axis_index("y")
    span = jnp.float32(L)
    decay = jnp.exp(-span * rate)
    zero = jnp.zeros((R, CH), F32)

    def moments(i):
        packed = msg_ref[i, MOMENT_ROW:SUM_ROW]
        moved = [pltpu.roll(packed, lax.rem(y + 4 - k, 4) * SHARE, 1) for k in range(4)]
        return jnp.concatenate(moved[:2], axis=0), jnp.concatenate(moved[2:], axis=0)

    f, f1, h0, h1, own_f = zero, zero, zero, zero, zero
    sums = jnp.zeros((G, 128), F32)
    back_moments = []
    for i in range(NP):
        own_f = jnp.where(me == i, f, own_f)
        fwd, bwd = msg_ref[i, :R], msg_ref[i, R : 2 * R]
        fwd1, bwd1 = moments(i)
        back_moments.append(bwd1)
        h0 = h0 + f * bwd
        h1 = h1 + f * bwd1 + f1 * bwd
        f1 = decay * (f1 + span * f) + fwd1
        f = decay * f + fwd
        sums = sums + msg_ref[i, SUM_ROW:]
    b, b1, own_b = zero, zero, zero
    for i in reversed(range(NP)):
        own_b = jnp.where(me == i, b, own_b)
        b1 = decay * (b1 + span * b) + back_moments[i]
        b = decay * b + msg_ref[i, R : 2 * R]
    carry_ref[:R] = own_f
    carry_ref[R:] = own_b
    mine = iota((R, CH), 1) // SHARE == y
    sums = sums + group_sums(jnp.where(mine, h0, 0.0), jnp.where(mine, h1, 0.0))
    share = share_of(f, b, f1, b1)
    z = lax.axis_index("z")
    for i in range(NZ):
        out_ref[i, :R] = jnp.where(z < i, f, b)
        out_ref[i, R : 2 * R] = share
        out_ref[i, 2 * R :] = sums


def share_of(f, b, f1, b1):
    start = lax.axis_index("y") * SHARE
    lane = iota((R, CH), 1)
    out = jnp.zeros((R, CH), F32)
    for k, state in enumerate((f, b, f1, b1)):
        moved = pltpu.roll(state, lax.rem(k * SHARE + CH - start, CH), 1)
        out = jnp.where(lane // SHARE == k, moved, out)
    return out


def final_kernel(msg_ref, table_ref, plane_ref, carry_ref, param_ref, skip_ref):
    inv = 1.0 / table_ref[0]
    rate = by_mode_and_channel(inv)
    me = plane_index().astype(F32)
    z = lax.axis_index("z")
    y = lax.axis_index("y")
    span = jnp.float32(L * NP)
    decay = jnp.exp(-span * rate)
    share_decay = pltpu.roll(decay, lax.rem(CH - y * SHARE, CH), 1)
    zero = jnp.zeros((R, CH), F32)
    own_f, own_b, f, f1, h0, h1 = zero, zero, zero, zero, zero, zero
    sums = jnp.zeros((G, 128), F32)
    for i in range(NZ):
        own_f = jnp.where(i < z, decay * own_f + msg_ref[i, :R], own_f)
        part = msg_ref[i, R : 2 * R]
        back = pltpu.roll(part, CH - SHARE, 1)
        f1_part = pltpu.roll(part, CH - 2 * SHARE, 1)
        b1_part = pltpu.roll(part, CH - 3 * SHARE, 1)
        h0 = h0 + f * back
        h1 = h1 + f * b1_part + f1 * back
        f1 = share_decay * (f1 + span * f) + f1_part
        f = share_decay * f + part
        sums = sums + msg_ref[i, 2 * R :]
    for i in reversed(range(NZ)):
        own_b = jnp.where(i > z, decay * own_b + msg_ref[i, :R], own_b)
    carry_ref[:R] = plane_ref[:R] + jnp.exp(-(L * me) * rate) * own_f
    carry_ref[R:] = plane_ref[R:] + jnp.exp(-(L * (NP - 1 - me)) * rate) * own_b
    pick = ones_where(iota((G, CH), 1) // M + y * (SHARE // M) == iota((G, CH), 0)) * ones_where(iota((G, CH), 1) < SHARE)
    mine = iota((R, CH), 1) < SHARE
    pairs = jnp.concatenate([jnp.where(mine, h0, 0.0), jnp.where(mine, h1, 0.0)], axis=0)
    whole = dot(pick, pairs, 1, 1)
    whole = whole + sums[:, : 2 * R]
    scale = 1.0 / math.sqrt(L * NP * NZ * M)
    h0, h1 = whole[:, :R], whole[:, R:]
    root = jnp.sqrt(2.0 * inv) * (1.0 / math.sqrt(R))
    params = jnp.concatenate(
        [
            h0 * root * scale,
            table_ref[1] * root * (h1 * inv - 0.5 * h0) * scale,
            jnp.zeros((G, 128 - 2 * R), F32),
        ],
        axis=1,
    )
    group = iota((G, 128), 0) - 2 * y
    params = jnp.where(group == 0, params, 0.0) + jnp.where(group == 1, pltpu.roll(params, 2 * R, 1), 0.0)
    params = jnp.sum(params, axis=0, keepdims=True)
    for i in range(PEERS):
        param_ref[i] = params
    lane = iota((128, 128), 1)
    row = iota((128, 128), 0)
    spread = dot(sums, ones_where(row - 2 * R == lane % M) * ones_where(row >= 2 * R) * ones_where(row < 3 * R))
    spread = jnp.where(iota((G, CH), 1) // M == iota((G, CH), 0), spread, 0.0)
    skip_ref[...] = jnp.sum(spread, axis=0, keepdims=True) * (1.0 / math.sqrt(L * NP * NZ))


def gather_kernel(part_ref, residue_ref, time_ref):
    rows = part_ref[...].reshape(PEERS, 128)
    lane = iota((128, 4 * G), 0)
    group = iota((128, 4 * G), 1)
    spread = jnp.concatenate([rows, jnp.zeros((128 - PEERS, 128), F32)], axis=0)
    out = jnp.zeros((2 * R, 4 * G), F32)
    for b in range(2):
        pick = ones_where(iota((2 * R, 128), 1) == iota((2 * R, 128), 0) + 2 * R * b)
        part = dot(pick, spread, 1, 1)
        out = out + dot(part, ones_where(group == 2 * lane + b))
    residue_ref[...] = out[:R]
    time_ref[...] = out[R:]


def gather_groups():
    groups = []
    index = lambda zh, z, y, core: ((zh * NZ + z) * 4 + y) * 2 + core
    for z in range(NZ):
        planes = {0: z, 1: (z + 4) % NZ}
        groups.append([index(zh, planes[zh], y, core) for zh in range(2) for core in range(2) for y in range(4)])
    return groups


def output_kernel(
    q_hbm, k_hbm, v_hbm, ct_hbm, fwd_ref, bwd_ref, head_ref, tail_ref, carry_ref,
    out_ref, gq_ref, gk_ref, gv_ref, q_ref, k_ref, v_ref, ct_ref, sems,
):
    fetch(((q_hbm, q_ref), (k_hbm, k_ref), (v_hbm, v_ref), (ct_hbm, ct_ref)), sems)
    mixed = fwd_ref[...] + dot(spread_states(carry_ref[:R]), head_ref[...], 0, 0)
    grad_product = bwd_ref[...] + dot(spread_states(carry_ref[R:]), tail_ref[...], 0, 0)
    out_ref[...] = (v_ref[...].astype(F32) * mixed).astype(jnp.bfloat16)
    gv_ref[...] = (ct_ref[...].astype(F32) * mixed).astype(jnp.bfloat16)
    gq_ref[...] = (grad_product * k_ref[...].astype(F32)).astype(jnp.bfloat16)
    gk_ref[...] = (grad_product * q_ref[...].astype(F32)).astype(jnp.bfloat16)


def shape(*dims, dtype=F32):
    return jax.ShapeDtypeStruct(dims, dtype)


def call(kernel, outs, flops, name, vmem=32 * 1024 * 1024, **options):
    return pl.pallas_call(
        kernel,
        out_shape=outs,
        name=name,
        cost_estimate=pl.CostEstimate(flops=flops, bytes_accessed=500_000, transcendentals=0),
        compiler_params=pltpu.CompilerParams(vmem_limit_bytes=vmem),
        **options,
    )


def per_device(queries, key_inputs, value_inputs, skip_gain, residue, timescale, cotangent):
    arrays = (queries, key_inputs, value_inputs, cotangent)
    hbm = pl.BlockSpec(memory_space=pltpu.HBM)
    local = pl.BlockSpec(memory_space=pltpu.VMEM)
    blocks = [pltpu.VMEM((CH, L), jnp.bfloat16)] * 4
    small = pltpu.VMEM((G, R), F32)
    message, table = call(
        local_kernel,
        (shape(NP, ROWS, 128), shape(2, G, R)),
        10**8,
        "local_states",
        vmem=62914560,
        in_specs=[hbm] * 6,
        scratch_shapes=[*blocks, small, small, pltpu.SemaphoreType.DMA((6,))],
    )(*arrays, timescale, residue)
    plane_states = lax.all_to_all(message, ("y", "x"), 0, 0)
    tables = call(
        conv_kernel,
        (shape(128, 128),) * 4,
        10**8,
        "local_conv",
        in_specs=[hbm] * 5 + [local],
        scratch_shapes=[*blocks, pltpu.VMEM((1, CH), F32), pltpu.SemaphoreType.DMA((5,))],
    )(*arrays, skip_gain.reshape(1, CH), table)
    totals, plane_carry = call(plane_kernel, (shape(NZ, Z_ROWS, 128), shape(2 * R, CH)), 10**7, "plane_scan")(
        plane_states, table
    )
    z_states = lax.all_to_all(totals, "z", 0, 0)
    carry, params, grad_skip = call(
        final_kernel, (shape(2 * R, CH), shape(PEERS, 1, 128), shape(1, CH)), 10**7, "z_scan"
    )(z_states, table, plane_carry)
    params = lax.all_to_all(params, ("zh", "z", "y", "core"), 0, 0, axis_index_groups=gather_groups())
    output, grad_queries, grad_keys, grad_values = call(
        output_kernel,
        (shape(CH, L, dtype=jnp.bfloat16),) * 4,
        10**8,
        "outputs",
        in_specs=[hbm] * 4 + [local] * 5,
        scratch_shapes=[*blocks, pltpu.SemaphoreType.DMA((4,))],
    )(*arrays, *tables, carry)
    grad_residue, grad_time = call(gather_kernel, (shape(R, 4 * G),) * 2, 10**6, "gather")(params)
    return (
        output,
        grad_queries,
        grad_keys,
        grad_values,
        grad_skip.reshape(CH),
        grad_residue.T,
        grad_time.T,
    )


def solution(mesh):
    grid = Mesh(mesh.devices.reshape(NZ, 4, 4, 2, 2), ("z", "y", "x", "zh", "core"))
    seq = ("z", "y", "x")
    ch = ("zh", "core")
    return jax.shard_map(
        per_device,
        mesh=grid,
        in_specs=(P(ch, seq), P(ch, seq), P(ch, seq), P(ch), P(ch, None), P(ch, None), P(ch, seq)),
        out_specs=(P(ch, seq), P(ch, seq), P(ch, seq), P(ch, seq), P(ch), P(), P()),
        check_vma=False,
    )
```

```python
import math

import jax
import jax.numpy as jnp
from jax import lax
from jax.experimental import pallas as pl
from jax.experimental.pallas import tpu as pltpu
from jax.sharding import Mesh, PartitionSpec as P

F32 = jnp.float32
HI = lax.Precision.HIGHEST
L = 128
CH = 128
G = 8
R = 16
M = 16
MOMENT_ROW = 2 * R
SUM_ROW = MOMENT_ROW + R // 2
ROWS = SUM_ROW + G
NP = 16
NZ = 8
SHARE = CH // 4
Z_ROWS = 2 * R + G
PEERS = 16
PLANE_FIRST = 15
Z_FIRST = (7, 4)


def dot(a, b, ca=1, cb=0):
    return lax.dot_general(a, b, (((ca,), (cb,)), ((), ())), precision=HI, preferred_element_type=F32)


def halves(value):
    high = value.astype(jnp.bfloat16)
    return high, (value - high.astype(F32)).astype(jnp.bfloat16)


def dot3(a, b, ca=1, cb=0):
    (a_high, a_low), (b_high, b_low) = halves(a), halves(b)
    left = jnp.concatenate([a_high, a_high, a_low], axis=ca)
    right = jnp.concatenate([b_high, b_low, b_high], axis=cb)
    return lax.dot_general(left, right, (((ca,), (cb,)), ((), ())), preferred_element_type=F32)


def pick_dot(pick, b, ca=1, cb=0):
    pick = pick.astype(jnp.bfloat16)
    left = jnp.concatenate([pick, pick], axis=ca)
    right = jnp.concatenate(halves(b), axis=cb)
    return lax.dot_general(left, right, (((ca,), (cb,)), ((), ())), preferred_element_type=F32)


def pick_dot_right(a, pick):
    pick = pick.astype(jnp.bfloat16)
    left = jnp.concatenate(halves(a), axis=1)
    right = jnp.concatenate([pick, pick], axis=0)
    return lax.dot_general(left, right, (((1,), (0,)), ((), ())), preferred_element_type=F32)


def iota(shape, axis):
    return lax.broadcasted_iota(jnp.int32, shape, axis)


def ones_where(cond):
    return jnp.where(cond, jnp.float32(1), jnp.float32(0))


def by_mode_and_channel(table):
    pick = ones_where(iota((G, CH), 1) // M == iota((G, CH), 0))
    return dot(table, pick, 0, 0)


def by_group_mode(table):
    rows = jnp.concatenate([jnp.broadcast_to(table[g : g + 1], (R, R)) for g in range(G)], axis=0)
    rows = jnp.where(iota((G * R, R), 0) % R == iota((G * R, R), 1), rows, 0.0)
    return jnp.sum(rows, axis=1, keepdims=True)


def same_group():
    return iota((128, 128), 0) // M == iota((128, 128), 1) // M


def fold_states(full):
    own = jnp.where(same_group(), full, 0.0)
    return jnp.sum(own.reshape(G, R, CH), axis=0)


def spread_states(state):
    return jnp.where(same_group(), jnp.concatenate([state] * G, axis=0), 0.0)


def group_sums(h0, h1):
    pick = ones_where(iota((G, CH), 1) // M == iota((G, CH), 0))
    rows = jnp.concatenate([h0, h1, jnp.zeros((CH - 2 * R, CH), F32)], axis=0)
    return pick_dot(pick, rows, 1, 1)


def fetch(pairs, sems):
    copies = [pltpu.make_async_copy(src, dst, sems.at[i]) for i, (src, dst) in enumerate(pairs)]
    for copy in copies:
        copy.start()
    for copy in copies:
        copy.wait()


def local_kernel(
    q_hbm, k_hbm, v_hbm, ct_hbm, tau_hbm, res_hbm, msg_hbm, table_ref,
    q_ref, k_ref, v_ref, ct_ref, states_ref, packed_ref, sums_ref, sems, out_sems,
):
    fetch(
        (
            (tau_hbm, table_ref.at[0]),
            (q_hbm, q_ref),
            (k_hbm, k_ref),
            (v_hbm, v_ref),
            (ct_hbm, ct_ref),
            (res_hbm, table_ref.at[1]),
        ),
        sems,
    )
    product = q_ref[...].astype(F32) * k_ref[...].astype(F32)
    grad_mixed = ct_ref[...].astype(F32) * v_ref[...].astype(F32)
    rate = by_group_mode(1.0 / table_ref[0])
    lane = iota((128, 128), 1)
    row = iota((128, 128), 0)
    step = lane.astype(F32)
    decay = jnp.exp(-step * rate)
    left = jnp.float32(L) - step
    decay_end = jnp.exp(-left * rate)
    fwd = dot3(jnp.concatenate([decay_end, left * decay_end], axis=0), product, 1, 1)
    bwd = dot3(jnp.concatenate([decay, step * decay], axis=0), grad_mixed, 1, 1)
    states_ref[:R] = fold_states(fwd[:128])
    states_ref[R:] = fold_states(bwd[:128])
    copies = []

    def send(source, i, rows):
        copies.append(pltpu.make_async_copy(source, msg_hbm.at[plane_slot(i), rows], out_sems.at[len(copies)]))
        copies[-1].start()

    for i in range(NP):
        send(states_ref, i, slice(0, MOMENT_ROW))
    moments = (fold_states(fwd[128:]), fold_states(bwd[128:]))
    quarters = (moments[0][:8], moments[0][8:], moments[1][:8], moments[1][8:])
    for y in range(4):
        packed = jnp.zeros((8, CH), F32)
        for k, quarter in enumerate(quarters):
            packed = jnp.where(lane[:8] // SHARE == k, pltpu.roll(quarter, (k - y) % 4 * SHARE, 1), packed)
        packed_ref[y] = packed
    for i in range(NP):
        send(packed_ref.at[i // 4], i, slice(MOMENT_ROW, SUM_ROW))
    flipped = pick_dot_right(product, ones_where(lane + row == L - 1))
    inside = lane + row >= L - 1
    lags = []
    for g in range(G):
        c = slice(g * M, (g + 1) * M)
        outer = jnp.where(inside, dot3(flipped[c], grad_mixed[c], 0, 0), 0.0)
        lags.append(jnp.sum(pltpu.roll(outer, 1, 1, stride=1, stride_axis=0), axis=0, keepdims=True))
    lags = jnp.concatenate(lags, axis=0)
    lags = jnp.concatenate([lags, lags * step[:G]], axis=0)
    modal = dot3(lags, decay, 1, 1)
    modal = jnp.where(iota((2 * G, G * R), 0) % G == iota((2 * G, G * R), 1) // R, modal, 0.0)
    modal = jnp.concatenate([modal[:G], modal[G:]], axis=1)
    fold = iota((2 * G * R, 128), 0)
    fold = ones_where(fold % R + fold // (G * R) * R == iota((2 * G * R, 128), 1))
    skip = jnp.sum(grad_mixed * product, axis=1, keepdims=True)
    skip = jnp.where(row % M == lane - 2 * R, skip, 0.0)
    pick = ones_where(iota((G, CH), 1) // M == iota((G, CH), 0))
    sums_ref[...] = pick_dot_right(modal, fold) + pick_dot(pick, skip)
    for i in range(NP):
        send(sums_ref, i, slice(SUM_ROW, ROWS))
    for copy in copies:
        copy.wait()


def conv_kernel(
    q_hbm, k_hbm, v_hbm, ct_hbm, skip_hbm, table_ref, fwd_ref, bwd_ref, head_ref, tail_ref, q_ref, k_ref, v_ref, ct_ref, skip_ref, sems
):
    fetch(((q_hbm, q_ref), (k_hbm, k_ref), (v_hbm, v_ref), (ct_hbm, ct_ref), (skip_hbm, skip_ref)), sems)
    product = q_ref[...].astype(F32) * k_ref[...].astype(F32)
    grad_mixed = ct_ref[...].astype(F32) * v_ref[...].astype(F32)
    inv = 1.0 / table_ref[0]
    rate = by_group_mode(inv)
    gain = by_group_mode(table_ref[1] * jnp.sqrt(2.0 * inv) * (1.0 / math.sqrt(R)))
    lane = iota((128, 128), 1)
    row = iota((128, 128), 0)
    step = lane.astype(F32)
    head = gain * jnp.exp(-step * rate)
    head_ref[...] = head
    tail_ref[...] = gain * jnp.exp(-(jnp.float32(L) - step) * rate)
    taps = jnp.sum(head.reshape(G, R, L), axis=1)
    skip = jnp.sum(jnp.where(lane == row, skip_ref[...], 0.0), axis=1, keepdims=True)
    for g in range(G):
        c = slice(g * M, (g + 1) * M)
        table = pltpu.roll(jnp.broadcast_to(taps[g : g + 1], (L, L)), 0, 1, stride=1, stride_axis=0)
        table = jnp.where(lane >= row, table, 0.0)
        fwd_ref[c] = dot(product[c], table) + skip[c] * product[c]
        bwd_ref[c] = dot(grad_mixed[c], table, 1, 1) + skip[c] * grad_mixed[c]


def plane_index():
    return lax.axis_index("y") * 4 + lax.axis_index("x")


def plane_kernel(msg_ref, table_ref, out_ref, carry_ref):
    rate = by_mode_and_channel(1.0 / table_ref[0])
    me = plane_index()
    y = lax.axis_index("y")
    span = jnp.float32(L)
    decay = jnp.exp(-span * rate)
    zero = jnp.zeros((R, CH), F32)

    def moments(i):
        packed = msg_ref[plane_slot(i), MOMENT_ROW:SUM_ROW]
        moved = [pltpu.roll(packed, lax.rem(y + 4 - k, 4) * SHARE, 1) for k in range(4)]
        return jnp.concatenate(moved[:2], axis=0), jnp.concatenate(moved[2:], axis=0)

    f, f1, h0, h1, own_f = zero, zero, zero, zero, zero
    sums = jnp.zeros((G, 128), F32)
    back_moments = []
    for i in range(NP):
        own_f = jnp.where(me == i, f, own_f)
        fwd, bwd = msg_ref[plane_slot(i), :R], msg_ref[plane_slot(i), R : 2 * R]
        fwd1, bwd1 = moments(i)
        back_moments.append(bwd1)
        h0 = h0 + f * bwd
        h1 = h1 + f * bwd1 + f1 * bwd
        f1 = decay * (f1 + span * f) + fwd1
        f = decay * f + fwd
        sums = sums + msg_ref[plane_slot(i), SUM_ROW:]
    b, b1, own_b = zero, zero, zero
    for i in reversed(range(NP)):
        own_b = jnp.where(me == i, b, own_b)
        b1 = decay * (b1 + span * b) + back_moments[i]
        b = decay * b + msg_ref[plane_slot(i), R : 2 * R]
    carry_ref[:R] = own_f
    carry_ref[R : 2 * R] = own_b
    carry_ref[2 * R :] = rate
    mine = iota((R, CH), 1) // SHARE == y
    sums = sums + group_sums(jnp.where(mine, h0, 0.0), jnp.where(mine, h1, 0.0))
    share = share_of(f, b, f1, b1)
    z = lax.axis_index("z")
    for i in range(NZ):
        out_ref[z_slot(i), :R] = jnp.where(z < i, f, b)
        out_ref[z_slot(i), R : 2 * R] = share
        out_ref[z_slot(i), 2 * R :] = sums


def share_of(f, b, f1, b1):
    start = lax.axis_index("y") * SHARE
    lane = iota((R, CH), 1)
    out = jnp.zeros((R, CH), F32)
    for k, state in enumerate((f, b, f1, b1)):
        moved = pltpu.roll(state, lax.rem(k * SHARE + CH - start, CH), 1)
        out = jnp.where(lane // SHARE == k, moved, out)
    return out


def final_kernel(msg_ref, table_ref, plane_ref, param_ref):
    inv = 1.0 / table_ref[0]
    y = lax.axis_index("y")
    span = jnp.float32(L * NP)
    decay = jnp.exp(-span * pltpu.roll(plane_ref[2 * R :], lax.rem(CH - y * SHARE, CH), 1))
    zero = jnp.zeros((R, CH), F32)
    f, f1, h0, h1 = zero, zero, zero, zero
    sums = jnp.zeros((G, 128), F32)
    for i in range(NZ):
        part = msg_ref[z_slot(i), R : 2 * R]
        back = pltpu.roll(part, CH - SHARE, 1)
        f1_part = pltpu.roll(part, CH - 2 * SHARE, 1)
        b1_part = pltpu.roll(part, CH - 3 * SHARE, 1)
        h0 = h0 + f * back
        h1 = h1 + f * b1_part + f1 * back
        f1 = decay * (f1 + span * f) + f1_part
        f = decay * f + part
        sums = sums + msg_ref[z_slot(i), 2 * R :]
    pick = ones_where(iota((G, CH), 1) // M + y * (SHARE // M) == iota((G, CH), 0)) * ones_where(iota((G, CH), 1) < SHARE)
    mine = iota((R, CH), 1) < SHARE
    pairs = jnp.concatenate([jnp.where(mine, h0, 0.0), jnp.where(mine, h1, 0.0)], axis=0)
    whole = pick_dot(pick, pairs, 1, 1) + sums[:, : 2 * R]
    scale = 1.0 / math.sqrt(L * NP * NZ * M)
    h0, h1 = whole[:, :R], whole[:, R:]
    root = jnp.sqrt(2.0 * inv) * (scale / math.sqrt(R))
    params = jnp.concatenate(
        [h0 * root, table_ref[1] * root * (h1 * inv - 0.5 * h0), jnp.zeros((G, 128 - 2 * R), F32)], axis=1
    )
    group = iota((G, 128), 0) - 2 * y
    params = jnp.where(group == 0, params, 0.0) + jnp.where(group == 1, pltpu.roll(params, 2 * R, 1), 0.0)
    params = jnp.sum(params, axis=0, keepdims=True)
    for i in range(PEERS):
        param_ref[i] = params


def gather_kernel(part_ref, residue_ref, time_ref):
    rows = part_ref[...].reshape(PEERS, 128)
    columns = jnp.concatenate([rows, jnp.zeros((128 - PEERS, 128), F32)], axis=0).T
    peer = iota((128, 4 * G), 0)
    group = iota((128, 4 * G), 1)
    y, core, zh = peer % 4, peer // 4 % 2, 1 - peer // 8
    first = (zh * 2 + core) * G + 2 * y
    out = jnp.zeros((2 * R, 4 * G), F32)
    for b in range(2):
        place = ones_where((group == first + b) & (peer < PEERS)).astype(jnp.bfloat16)
        for half in halves(columns[2 * R * b : 2 * R * (b + 1)]):
            out = out + lax.dot_general(half, place, (((1,), (0,)), ((), ())), preferred_element_type=F32)
    residue_ref[...] = out[:R]
    time_ref[...] = out[R:]


def plane_slot(p):
    return (p - PLANE_FIRST) % NP


def z_slot(z):
    first = jnp.where(lax.axis_index("zh") == 1, Z_FIRST[1], Z_FIRST[0])
    return lax.rem(z + NZ - first, NZ)


def plane_groups():
    return [[(PLANE_FIRST + i) % NP for i in range(NP)]]


def z_groups():
    return [[zh * NZ + (first + i) % NZ for i in range(NZ)] for zh, first in enumerate(Z_FIRST)]


def gather_groups():
    groups = []
    index = lambda zh, z, y, core: ((zh * NZ + z) * 4 + y) * 2 + core
    for z in range(NZ):
        planes = {0: z, 1: (z + 4) % NZ}
        groups.append([index(zh, planes[zh], y, core) for zh in (1, 0) for core in range(2) for y in range(4)])
    return groups


def output_kernel(
    q_hbm, k_hbm, v_hbm, ct_hbm, fwd_ref, bwd_ref, head_ref, tail_ref, msg_ref, plane_ref,
    out_ref, gq_ref, gk_ref, gv_ref, skip_ref, q_ref, k_ref, v_ref, ct_ref, sems,
):
    fetch(((q_hbm, q_ref), (k_hbm, k_ref), (v_hbm, v_ref), (ct_hbm, ct_ref)), sems)
    rate = plane_ref[2 * R :]
    z = lax.axis_index("z")
    me = plane_index().astype(F32)
    decay = jnp.exp(-jnp.float32(L * NP) * rate)
    own_f = jnp.zeros((R, CH), F32)
    own_b = own_f
    sums = jnp.zeros((G, 128), F32)
    for i in range(NZ):
        own_f = jnp.where(i < z, decay * own_f + msg_ref[z_slot(i), :R], own_f)
        sums = sums + msg_ref[z_slot(i), 2 * R :]
    for i in reversed(range(NZ)):
        own_b = jnp.where(i > z, decay * own_b + msg_ref[z_slot(i), :R], own_b)
    own_f = plane_ref[:R] + jnp.exp(-(L * me) * rate) * own_f
    own_b = plane_ref[R : 2 * R] + jnp.exp(-(L * (NP - 1 - me)) * rate) * own_b
    lane = iota((128, 128), 1)
    row = iota((128, 128), 0)
    spread = dot(sums, ones_where((row - 2 * R == lane % M) & (row >= 2 * R) & (row < 3 * R)))
    spread = jnp.where(iota((G, CH), 1) // M == iota((G, CH), 0), spread, 0.0)
    skip_ref[...] = jnp.sum(spread, axis=0, keepdims=True) * (1.0 / math.sqrt(L * NP * NZ))
    mixed = fwd_ref[...] + dot3(spread_states(own_f), head_ref[...], 0, 0)
    grad_product = bwd_ref[...] + dot3(spread_states(own_b), tail_ref[...], 0, 0)
    out_ref[...] = (v_ref[...].astype(F32) * mixed).astype(jnp.bfloat16)
    gv_ref[...] = (ct_ref[...].astype(F32) * mixed).astype(jnp.bfloat16)
    gq_ref[...] = (grad_product * k_ref[...].astype(F32)).astype(jnp.bfloat16)
    gk_ref[...] = (grad_product * q_ref[...].astype(F32)).astype(jnp.bfloat16)


def shape(*dims, dtype=F32):
    return jax.ShapeDtypeStruct(dims, dtype)


def call(kernel, outs, flops, name, vmem=32 * 1024 * 1024, **options):
    return pl.pallas_call(
        kernel,
        out_shape=outs,
        name=name,
        cost_estimate=pl.CostEstimate(flops=flops, bytes_accessed=500_000, transcendentals=0),
        compiler_params=pltpu.CompilerParams(vmem_limit_bytes=vmem),
        **options,
    )


def per_device(queries, key_inputs, value_inputs, skip_gain, residue, timescale, cotangent):
    arrays = (queries, key_inputs, value_inputs, cotangent)
    hbm = pl.BlockSpec(memory_space=pltpu.HBM)
    local = pl.BlockSpec(memory_space=pltpu.VMEM)
    blocks = [pltpu.VMEM((CH, L), jnp.bfloat16)] * 4
    message, table = call(
        local_kernel,
        (shape(NP, ROWS, 128), shape(2, G, R)),
        10**8,
        "local_states",
        vmem=60 * 1024 * 1024,
        in_specs=[hbm] * 6,
        out_specs=(hbm, local),
        scratch_shapes=[
            *blocks,
            pltpu.VMEM((2 * R, CH), F32),
            pltpu.VMEM((4, 8, CH), F32),
            pltpu.VMEM((G, CH), F32),
            pltpu.SemaphoreType.DMA((6,)),
            pltpu.SemaphoreType.DMA((3 * NP,)),
        ],
    )(*arrays, timescale, residue)
    plane_states = lax.all_to_all(message, ("y", "x"), 0, 0, axis_index_groups=plane_groups())
    tables = call(
        conv_kernel,
        (shape(128, 128),) * 4,
        10**8,
        "local_conv",
        in_specs=[hbm] * 5 + [local],
        scratch_shapes=[*blocks, pltpu.VMEM((1, CH), F32), pltpu.SemaphoreType.DMA((5,))],
    )(*arrays, skip_gain.reshape(1, CH), table)
    totals, plane_carry = call(plane_kernel, (shape(NZ, Z_ROWS, 128), shape(3 * R, CH)), 10**7, "plane_scan")(
        plane_states, table
    )
    z_states = lax.all_to_all(totals, ("zh", "z"), 0, 0, axis_index_groups=z_groups())
    params = call(final_kernel, shape(PEERS, 1, 128), 10**7, "z_scan")(z_states, table, plane_carry)
    params = lax.all_to_all(params, ("zh", "z", "y", "core"), 0, 0, axis_index_groups=gather_groups())
    output, grad_queries, grad_keys, grad_values, grad_skip = call(
        output_kernel,
        (*(shape(CH, L, dtype=jnp.bfloat16),) * 4, shape(1, CH)),
        10**8,
        "outputs",
        in_specs=[hbm] * 4 + [local] * 6,
        scratch_shapes=[*blocks, pltpu.SemaphoreType.DMA((4,))],
    )(*arrays, *tables, z_states, plane_carry)
    grad_residue, grad_time = call(gather_kernel, (shape(R, 4 * G),) * 2, 10**6, "gather")(params)
    return (
        output,
        grad_queries,
        grad_keys,
        grad_values,
        grad_skip.reshape(CH),
        grad_residue.T,
        grad_time.T,
    )


def solution(mesh):
    grid = Mesh(mesh.devices.reshape(NZ, 4, 4, 2, 2), ("z", "y", "x", "zh", "core"))
    seq = ("z", "y", "x")
    ch = ("zh", "core")
    return jax.shard_map(
        per_device,
        mesh=grid,
        in_specs=(P(ch, seq), P(ch, seq), P(ch, seq), P(ch), P(ch, None), P(ch, None), P(ch, seq)),
        out_specs=(P(ch, seq), P(ch, seq), P(ch, seq), P(ch, seq), P(ch), P(), P()),
        check_vma=False,
    )
```

```python
import math

import jax
import jax.numpy as jnp
from jax import lax
from jax.experimental import pallas as pl
from jax.experimental.pallas import tpu as pltpu
from jax.sharding import Mesh, PartitionSpec as P

F32 = jnp.float32
HI = lax.Precision.HIGHEST
L = 128
CH = 128
G = 8
R = 16
M = 16
MOMENT_ROW = 2 * R
SUM_ROW = MOMENT_ROW + R
ROWS = SUM_ROW + G
NP = 16
NZ = 8
SHARE = CH // 2
Z_ROWS = 3 * R
PEERS = 8
PLANE_FIRST = 15
Z_FIRST = (7, 3)


def dot(a, b, ca=1, cb=0):
    return lax.dot_general(a, b, (((ca,), (cb,)), ((), ())), precision=HI, preferred_element_type=F32)


def halves(value):
    high = value.astype(jnp.bfloat16)
    return high, (value - high.astype(F32)).astype(jnp.bfloat16)


def dot3(a, b, ca=1, cb=0):
    (a_high, a_low), (b_high, b_low) = halves(a), halves(b)
    left = jnp.concatenate([a_high, a_high, a_low], axis=ca)
    right = jnp.concatenate([b_high, b_low, b_high], axis=cb)
    return lax.dot_general(left, right, (((ca,), (cb,)), ((), ())), preferred_element_type=F32)


def pick_dot(pick, b, ca=1, cb=0):
    pick = pick.astype(jnp.bfloat16)
    left = jnp.concatenate([pick, pick], axis=ca)
    right = jnp.concatenate(halves(b), axis=cb)
    return lax.dot_general(left, right, (((ca,), (cb,)), ((), ())), preferred_element_type=F32)


def pick_dot_right(a, pick):
    pick = pick.astype(jnp.bfloat16)
    left = jnp.concatenate(halves(a), axis=1)
    right = jnp.concatenate([pick, pick], axis=0)
    return lax.dot_general(left, right, (((1,), (0,)), ((), ())), preferred_element_type=F32)


def iota(shape, axis):
    return lax.broadcasted_iota(jnp.int32, shape, axis)


def ones_where(cond):
    return jnp.where(cond, jnp.float32(1), jnp.float32(0))


def by_mode_and_channel(table):
    pick = ones_where(iota((G, CH), 1) // M == iota((G, CH), 0))
    return dot(table, pick, 0, 0)


def by_group_mode(table):
    rows = jnp.concatenate([jnp.broadcast_to(table[g : g + 1], (R, R)) for g in range(G)], axis=0)
    rows = jnp.where(iota((G * R, R), 0) % R == iota((G * R, R), 1), rows, 0.0)
    return jnp.sum(rows, axis=1, keepdims=True)


def same_group():
    return iota((128, 128), 0) // M == iota((128, 128), 1) // M


def fold_states(full):
    own = jnp.where(same_group(), full, 0.0)
    return jnp.sum(own.reshape(G, R, CH), axis=0)


def spread_states(state):
    return jnp.where(same_group(), jnp.concatenate([state] * G, axis=0), 0.0)


def front_sums(h0, h1, half):
    lane = iota((G, CH), 1)
    pick = ones_where((lane // M + half * (SHARE // M) == iota((G, CH), 0)) & (lane < SHARE))
    front = iota((R, CH), 1) < SHARE
    rows = [jnp.where(front, h0, 0.0), jnp.where(front, h1, 0.0), jnp.zeros((CH - 2 * R, CH), F32)]
    return pick_dot(pick, jnp.concatenate(rows, axis=0), 1, 1)


def fetch(pairs, sems):
    copies = [pltpu.make_async_copy(src, dst, sems.at[i]) for i, (src, dst) in enumerate(pairs)]
    for copy in copies:
        copy.start()
    for copy in copies:
        copy.wait()


def side_by_side(a, b, half):
    a, b = (a, pltpu.roll(b, SHARE, 1)) if half == 0 else (pltpu.roll(a, SHARE, 1), b)
    return jnp.where(iota((R, CH), 1) < SHARE, a, b)


def local_kernel(
    q_hbm, k_hbm, v_hbm, ct_hbm, tau_hbm, msg_hbm,
    q_ref, k_ref, v_ref, ct_ref, tau_ref, states_ref, packed_ref, sums_ref, sems, out_sems,
):
    fetch(
        (
            (tau_hbm, tau_ref),
            (q_hbm, q_ref),
            (k_hbm, k_ref),
            (v_hbm, v_ref),
            (ct_hbm, ct_ref),
        ),
        sems,
    )
    product = q_ref[...].astype(F32) * k_ref[...].astype(F32)
    grad_mixed = ct_ref[...].astype(F32) * v_ref[...].astype(F32)
    rate = by_group_mode(1.0 / tau_ref[...])
    lane = iota((128, 128), 1)
    row = iota((128, 128), 0)
    step = lane.astype(F32)
    decay = jnp.exp(-step * rate)
    left = jnp.float32(L) - step
    decay_end = jnp.exp(-left * rate)
    fwd = dot3(jnp.concatenate([decay_end, left * decay_end], axis=0), product, 1, 1)
    bwd = dot3(jnp.concatenate([decay, step * decay], axis=0), grad_mixed, 1, 1)
    states_ref[:R] = fold_states(fwd[:128])
    states_ref[R:] = fold_states(bwd[:128])
    copies = []

    def send(source, i, rows):
        copies.append(pltpu.make_async_copy(source, msg_hbm.at[plane_slot(i), rows], out_sems.at[len(copies)]))
        copies[-1].start()

    for i in range(NP):
        send(states_ref, i, slice(0, MOMENT_ROW))
    moments = (fold_states(fwd[128:]), fold_states(bwd[128:]))
    for half in range(2):
        packed_ref[half] = side_by_side(*moments, half)
    for i in range(NP):
        send(packed_ref.at[i // 4 % 2], i, slice(MOMENT_ROW, SUM_ROW))
    flipped = pick_dot_right(product, ones_where(lane + row == L - 1))
    inside = lane + row >= L - 1
    lags = []
    for g in range(G):
        c = slice(g * M, (g + 1) * M)
        outer = jnp.where(inside, dot3(flipped[c], grad_mixed[c], 0, 0), 0.0)
        lags.append(jnp.sum(pltpu.roll(outer, 1, 1, stride=1, stride_axis=0), axis=0, keepdims=True))
    lags = jnp.concatenate(lags, axis=0)
    lags = jnp.concatenate([lags, lags * step[:G]], axis=0)
    modal = dot3(lags, decay, 1, 1)
    modal = jnp.where(iota((2 * G, G * R), 0) % G == iota((2 * G, G * R), 1) // R, modal, 0.0)
    modal = jnp.concatenate([modal[:G], modal[G:]], axis=1)
    fold = iota((2 * G * R, 128), 0)
    fold = ones_where(fold % R + fold // (G * R) * R == iota((2 * G * R, 128), 1))
    skip = jnp.sum(grad_mixed * product, axis=1, keepdims=True)
    skip = jnp.where(row % M == lane - 2 * R, skip, 0.0)
    pick = ones_where(iota((G, CH), 1) // M == iota((G, CH), 0))
    sums_ref[...] = pick_dot_right(modal, fold) + pick_dot(pick, skip)
    for i in range(NP):
        send(sums_ref, i, slice(SUM_ROW, ROWS))
    for copy in copies:
        copy.wait()


def conv_kernel(
    q_hbm, k_hbm, v_hbm, ct_hbm, skip_hbm, tau_ref, res_ref, fwd_ref, bwd_ref, head_ref, tail_ref, rate_ref, q_ref, k_ref, v_ref, ct_ref, skip_ref, sems
):
    fetch(((q_hbm, q_ref), (k_hbm, k_ref), (v_hbm, v_ref), (ct_hbm, ct_ref), (skip_hbm, skip_ref)), sems)
    product = q_ref[...].astype(F32) * k_ref[...].astype(F32)
    grad_mixed = ct_ref[...].astype(F32) * v_ref[...].astype(F32)
    inv = 1.0 / tau_ref[...]
    rate_ref[...] = by_mode_and_channel(inv)
    rate = by_group_mode(inv)
    gain = by_group_mode(res_ref[...] * jnp.sqrt(2.0 * inv) * (1.0 / math.sqrt(R)))
    lane = iota((128, 128), 1)
    row = iota((128, 128), 0)
    step = lane.astype(F32)
    head = gain * jnp.exp(-step * rate)
    head_ref[...] = head
    tail_ref[...] = gain * jnp.exp(-(jnp.float32(L) - step) * rate)
    taps = jnp.sum(head.reshape(G, R, L), axis=1)
    skip = jnp.sum(jnp.where(lane == row, skip_ref[...], 0.0), axis=1, keepdims=True)
    for g in range(G):
        c = slice(g * M, (g + 1) * M)
        table = pltpu.roll(jnp.broadcast_to(taps[g : g + 1], (L, L)), 0, 1, stride=1, stride_axis=0)
        table = jnp.where(lane >= row, table, 0.0)
        fwd_ref[c] = dot(product[c], table) + skip[c] * product[c]
        bwd_ref[c] = dot(grad_mixed[c], table, 1, 1) + skip[c] * grad_mixed[c]


def plane_index():
    return lax.axis_index("y") * 4 + lax.axis_index("x")


def to_front(state, half):
    return pltpu.roll(state, half * SHARE, 1)


def plane_kernel(msg_ref, rate_ref, out_ref, carry_ref):
    rate = rate_ref[...]
    me = plane_index()
    half = lax.rem(lax.axis_index("y"), 2)
    span = jnp.float32(L)
    decay = jnp.exp(-span * rate)
    zero = jnp.zeros((R, CH), F32)
    front_decay = to_front(decay, half)
    f, g, f1, h0, h1, own_f = zero, zero, zero, zero, zero, zero
    sums = jnp.zeros((G, 128), F32)
    fronts = []
    for i in range(NP):
        at = plane_slot(i)
        own_f = jnp.where(me == i, f, own_f)
        fwd, fwd1 = msg_ref[at, :R], msg_ref[at, MOMENT_ROW:SUM_ROW]
        bwd, bwd1 = to_front(msg_ref[at, R : 2 * R], half), pltpu.roll(fwd1, SHARE, 1)
        fronts.append((bwd, bwd1))
        h0 = h0 + g * bwd
        h1 = h1 + g * bwd1 + f1 * bwd
        f1 = front_decay * (f1 + span * g) + fwd1
        g = front_decay * g + to_front(fwd, half)
        f = decay * f + fwd
        sums = sums + msg_ref[at, SUM_ROW:]
    b, e, b1, own_b = zero, zero, zero, zero
    for i in reversed(range(NP)):
        bwd, bwd1 = fronts[i]
        own_b = jnp.where(me == i, b, own_b)
        b1 = front_decay * (b1 + span * e) + bwd1
        e = front_decay * e + bwd
        b = decay * b + msg_ref[plane_slot(i), R : 2 * R]
    carry_ref[:R] = own_f
    carry_ref[R : 2 * R] = own_b
    sums = sums + front_sums(h0, h1, half)
    front = iota((R, CH), 1) < SHARE
    f1 = pltpu.roll(f1, SHARE, 1)
    sums = jnp.concatenate([pltpu.roll(sums, SHARE, 1), jnp.zeros((R - G, CH), F32)], axis=0)
    last = jnp.where(front, b1, sums)
    z = lax.axis_index("z")
    for i in range(NZ):
        above = z < i
        out_ref[z_slot(i), :R] = jnp.where(above, f, b)
        out_ref[z_slot(i), R : 2 * R] = jnp.where(front, jnp.where(above, e, g), f1)
        out_ref[z_slot(i), 2 * R :] = last


def final_kernel(msg_ref, tau_ref, res_ref, rate_ref, param_ref):
    inv = 1.0 / tau_ref[...]
    half = lax.rem(lax.axis_index("y"), 2)
    z = lax.axis_index("z")
    span = jnp.float32(L * NP)
    decay = jnp.exp(-span * to_front(rate_ref[...], half))
    zero = jnp.zeros((R, CH), F32)
    f, f1, h0, h1 = zero, zero, zero, zero
    sums = jnp.zeros((G, 128), F32)
    for i in range(NZ):
        at = z_slot(i)
        carry = to_front(msg_ref[at, :R], half)
        part = msg_ref[at, R : 2 * R]
        fwd, bwd = jnp.where(i < z, carry, part), jnp.where(i < z, part, carry)
        bwd1 = msg_ref[at, 2 * R :]
        h0 = h0 + f * bwd
        h1 = h1 + f * bwd1 + f1 * bwd
        f1 = decay * (f1 + span * f) + pltpu.roll(part, SHARE, 1)
        f = decay * f + fwd
        sums = sums + msg_ref[at, 2 * R : 2 * R + G]
    whole = front_sums(h0, h1, half) + pltpu.roll(sums, SHARE, 1)
    scale = 1.0 / math.sqrt(L * NP * NZ * M)
    h0, h1 = whole[:, :R], whole[:, R : 2 * R]
    root = jnp.sqrt(2.0 * inv) * (scale / math.sqrt(R))
    params = jnp.concatenate(
        [h0 * root, res_ref[...] * root * (h1 * inv - 0.5 * h0), jnp.zeros((G, 128 - 2 * R), F32)], axis=1
    )
    group = iota((G, 128), 0) - half * (G // 2)
    row = jnp.where(group == 0, params, 0.0)
    for k in range(1, G // 2):
        row = row + jnp.where(group == k, pltpu.roll(params, 2 * R * k, 1), 0.0)
    row = jnp.sum(row, axis=0, keepdims=True)
    for i in range(PEERS):
        param_ref[i] = row


def gather_kernel(part_ref, residue_ref, time_ref):
    rows = part_ref[...].reshape(PEERS, 128)
    columns = jnp.concatenate([rows, jnp.zeros((128 - PEERS, 128), F32)], axis=0).T
    peer = iota((128, 4 * G), 0)
    group = iota((128, 4 * G), 1)
    half, core, zh = 1 - peer % 2, peer // 2 % 2, 1 - peer // 4
    first = (zh * 2 + core) * G + half * (G // 2)
    out = jnp.zeros((2 * R, 4 * G), F32)
    for k in range(G // 2):
        place = ones_where((group == first + k) & (peer < PEERS)).astype(jnp.bfloat16)
        for part in halves(columns[2 * R * k : 2 * R * (k + 1)]):
            out = out + lax.dot_general(part, place, (((1,), (0,)), ((), ())), preferred_element_type=F32)
    residue_ref[...] = out[:R]
    time_ref[...] = out[R:]


def plane_slot(p):
    return (p - PLANE_FIRST) % NP


def z_slot(z):
    first = jnp.where(lax.axis_index("zh") == 1, Z_FIRST[1], Z_FIRST[0])
    return lax.rem(z + NZ - first, NZ)


def plane_groups():
    return [[(PLANE_FIRST + i) % NP for i in range(NP)]]


def z_groups():
    return [[zh * NZ + (first + i) % NZ for i in range(NZ)] for zh, first in enumerate(Z_FIRST)]


def gather_groups():
    groups = []
    index = lambda zh, z, y, core: ((zh * NZ + z) * 4 + y) * 2 + core
    for z in range(NZ):
        planes = {0: z, 1: (z + 4) % NZ}
        for pair in (0, 2):
            groups.append([index(zh, planes[zh], pair + half, core) for zh in (1, 0) for core in (0, 1) for half in (1, 0)])
    return groups


def output_kernel(
    q_hbm, k_hbm, v_hbm, ct_hbm, fwd_ref, bwd_ref, head_ref, tail_ref, msg_ref, plane_ref, rate_ref,
    out_ref, gq_ref, gk_ref, gv_ref, skip_ref, q_ref, k_ref, v_ref, ct_ref, sems,
):
    fetch(((q_hbm, q_ref), (k_hbm, k_ref), (v_hbm, v_ref), (ct_hbm, ct_ref)), sems)
    rate = rate_ref[...]
    z = lax.axis_index("z")
    me = plane_index().astype(F32)
    decay = jnp.exp(-jnp.float32(L * NP) * rate)
    own_f = jnp.zeros((R, CH), F32)
    own_b = own_f
    sums = jnp.zeros((G, 128), F32)
    for i in range(NZ):
        own_f = jnp.where(i < z, decay * own_f + msg_ref[z_slot(i), :R], own_f)
        sums = sums + msg_ref[z_slot(i), 2 * R : 2 * R + G]
    for i in reversed(range(NZ)):
        own_b = jnp.where(i > z, decay * own_b + msg_ref[z_slot(i), :R], own_b)
    own_f = plane_ref[:R] + jnp.exp(-(L * me) * rate) * own_f
    own_b = plane_ref[R : 2 * R] + jnp.exp(-(L * (NP - 1 - me)) * rate) * own_b
    lane = iota((128, 128), 1)
    row = iota((128, 128), 0)
    spread = dot(sums, ones_where((row - 2 * R - SHARE == lane % M) & (row >= 2 * R + SHARE) & (row < 3 * R + SHARE)))
    spread = jnp.where(iota((G, CH), 1) // M == iota((G, CH), 0), spread, 0.0)
    skip_ref[...] = jnp.sum(spread, axis=0, keepdims=True) * (1.0 / math.sqrt(L * NP * NZ))
    mixed = fwd_ref[...] + dot3(spread_states(own_f), head_ref[...], 0, 0)
    grad_product = bwd_ref[...] + dot3(spread_states(own_b), tail_ref[...], 0, 0)
    out_ref[...] = (v_ref[...].astype(F32) * mixed).astype(jnp.bfloat16)
    gv_ref[...] = (ct_ref[...].astype(F32) * mixed).astype(jnp.bfloat16)
    gq_ref[...] = (grad_product * k_ref[...].astype(F32)).astype(jnp.bfloat16)
    gk_ref[...] = (grad_product * q_ref[...].astype(F32)).astype(jnp.bfloat16)


def shape(*dims, dtype=F32):
    return jax.ShapeDtypeStruct(dims, dtype)


def call(kernel, outs, flops, name, vmem=32 * 1024 * 1024, **options):
    return pl.pallas_call(
        kernel,
        out_shape=outs,
        name=name,
        cost_estimate=pl.CostEstimate(flops=flops, bytes_accessed=500_000, transcendentals=0),
        compiler_params=pltpu.CompilerParams(vmem_limit_bytes=vmem),
        **options,
    )


def per_device(queries, key_inputs, value_inputs, skip_gain, residue, timescale, cotangent):
    arrays = (queries, key_inputs, value_inputs, cotangent)
    hbm = pl.BlockSpec(memory_space=pltpu.HBM)
    local = pl.BlockSpec(memory_space=pltpu.VMEM)
    blocks = [pltpu.VMEM((CH, L), jnp.bfloat16)] * 4
    message = call(
        local_kernel,
        shape(NP, ROWS, 128),
        10**8,
        "local_states",
        vmem=60 * 1024 * 1024,
        in_specs=[hbm] * 5,
        out_specs=hbm,
        scratch_shapes=[
            *blocks,
            pltpu.VMEM((G, R), F32),
            pltpu.VMEM((2 * R, CH), F32),
            pltpu.VMEM((2, R, CH), F32),
            pltpu.VMEM((G, CH), F32),
            pltpu.SemaphoreType.DMA((5,)),
            pltpu.SemaphoreType.DMA((3 * NP,)),
        ],
    )(*arrays, timescale)
    plane_states = lax.all_to_all(message, ("y", "x"), 0, 0, axis_index_groups=plane_groups())
    *tables, rate = call(
        conv_kernel,
        (*(shape(128, 128),) * 4, shape(R, CH)),
        10**8,
        "local_conv",
        in_specs=[hbm] * 5 + [local] * 2,
        scratch_shapes=[*blocks, pltpu.VMEM((1, CH), F32), pltpu.SemaphoreType.DMA((5,))],
    )(*arrays, skip_gain.reshape(1, CH), timescale, residue)
    totals, plane_carry = call(plane_kernel, (shape(NZ, Z_ROWS, 128), shape(2 * R, CH)), 10**7, "plane_scan")(
        plane_states, rate
    )
    z_states = lax.all_to_all(totals, ("zh", "z"), 0, 0, axis_index_groups=z_groups())
    params = call(final_kernel, shape(PEERS, 1, 128), 10**7, "z_scan")(z_states, timescale, residue, rate)
    params = lax.all_to_all(params, ("zh", "z", "y", "core"), 0, 0, axis_index_groups=gather_groups())
    output, grad_queries, grad_keys, grad_values, grad_skip = call(
        output_kernel,
        (*(shape(CH, L, dtype=jnp.bfloat16),) * 4, shape(1, CH)),
        10**8,
        "outputs",
        in_specs=[hbm] * 4 + [local] * 7,
        scratch_shapes=[*blocks, pltpu.SemaphoreType.DMA((4,))],
    )(*arrays, *tables, z_states, plane_carry, rate)
    grad_residue, grad_time = call(gather_kernel, (shape(R, 4 * G),) * 2, 10**6, "gather")(params)
    return (
        output,
        grad_queries,
        grad_keys,
        grad_values,
        grad_skip.reshape(CH),
        grad_residue.T,
        grad_time.T,
    )


def solution(mesh):
    grid = Mesh(mesh.devices.reshape(NZ, 4, 4, 2, 2), ("z", "y", "x", "zh", "core"))
    seq = ("z", "y", "x")
    ch = ("zh", "core")
    return jax.shard_map(
        per_device,
        mesh=grid,
        in_specs=(P(ch, seq), P(ch, seq), P(ch, seq), P(ch), P(ch, None), P(ch, None), P(ch, seq)),
        out_specs=(P(ch, seq), P(ch, seq), P(ch, seq), P(ch, seq), P(ch), P(), P()),
        check_vma=False,
    )
```

```python
import math

import jax
import jax.numpy as jnp
from jax import lax
from jax.experimental import pallas as pl
from jax.experimental.pallas import tpu as pltpu
from jax.sharding import Mesh, PartitionSpec as P

F32 = jnp.float32
HI = lax.Precision.HIGHEST
L = 128
CH = 128
G = 8
R = 16
M = 16
MOMENT_ROW = 2 * R
SUM_ROW = MOMENT_ROW + R // 2
ROWS = SUM_ROW + G
NP = 16
NZ = 8
SHARE = CH // 4
Z_ROWS = 2 * R
PEERS = 16
PLANE_FIRST = 15
Z_FIRST = (7, 3)


def dot(a, b, ca=1, cb=0):
    return lax.dot_general(a, b, (((ca,), (cb,)), ((), ())), precision=HI, preferred_element_type=F32)


def halves(value):
    high = value.astype(jnp.bfloat16)
    return high, (value - high.astype(F32)).astype(jnp.bfloat16)


def dot3(a, b, ca=1, cb=0):
    (a_high, a_low), (b_high, b_low) = halves(a), halves(b)
    left = jnp.concatenate([a_high, a_high, a_low], axis=ca)
    right = jnp.concatenate([b_high, b_low, b_high], axis=cb)
    return lax.dot_general(left, right, (((ca,), (cb,)), ((), ())), preferred_element_type=F32)


def pick_dot(pick, b, ca=1, cb=0):
    pick = pick.astype(jnp.bfloat16)
    left = jnp.concatenate([pick, pick], axis=ca)
    right = jnp.concatenate(halves(b), axis=cb)
    return lax.dot_general(left, right, (((ca,), (cb,)), ((), ())), preferred_element_type=F32)


def pick_dot_right(a, pick):
    pick = pick.astype(jnp.bfloat16)
    left = jnp.concatenate(halves(a), axis=1)
    right = jnp.concatenate([pick, pick], axis=0)
    return lax.dot_general(left, right, (((1,), (0,)), ((), ())), preferred_element_type=F32)


def iota(shape, axis):
    return lax.broadcasted_iota(jnp.int32, shape, axis)


def ones_where(cond):
    return jnp.where(cond, jnp.float32(1), jnp.float32(0))


def by_mode_and_channel(table):
    pick = ones_where(iota((G, CH), 1) // M == iota((G, CH), 0))
    return dot(table, pick, 0, 0)


def by_group_mode(table):
    rows = jnp.concatenate([jnp.broadcast_to(table[g : g + 1], (R, R)) for g in range(G)], axis=0)
    rows = jnp.where(iota((G * R, R), 0) % R == iota((G * R, R), 1), rows, 0.0)
    return jnp.sum(rows, axis=1, keepdims=True)


def same_group():
    return iota((128, 128), 0) // M == iota((128, 128), 1) // M


def fold_states(full):
    own = jnp.where(same_group(), full, 0.0)
    return jnp.sum(own.reshape(G, R, CH), axis=0)


def spread_states(state):
    return jnp.where(same_group(), jnp.concatenate([state] * G, axis=0), 0.0)


def front_sums(h0, h1, quarter):
    lane = iota((G, CH), 1)
    pick = ones_where((lane // M + quarter * (SHARE // M) == iota((G, CH), 0)) & (lane < SHARE))
    front = iota((R, CH), 1) < SHARE
    rows = [jnp.where(front, h0, 0.0), jnp.where(front, h1, 0.0), jnp.zeros((CH - 2 * R, CH), F32)]
    return pick_dot(pick, jnp.concatenate(rows, axis=0), 1, 1)


def fetch(pairs, sems):
    copies = [pltpu.make_async_copy(src, dst, sems.at[i]) for i, (src, dst) in enumerate(pairs)]
    for copy in copies:
        copy.start()
    for copy in copies:
        copy.wait()


def quarter_of(y, x):
    return y % 2 * 2 + x % 2


def pack_moments(a, b, quarter):
    packed = jnp.zeros((8, CH), F32)
    for k, piece in enumerate((a[:8], a[8:], b[:8], b[8:])):
        packed = jnp.where(iota((8, CH), 1) // SHARE == k, pltpu.roll(piece, (k - quarter) % 4 * SHARE, 1), packed)
    return packed


def unpack_moments(packed):
    moved = [packed] + [pltpu.roll(packed, CH - k * SHARE, 1) for k in range(1, 4)]
    return jnp.concatenate(moved[:2], axis=0), jnp.concatenate(moved[2:], axis=0)


def local_kernel(
    q_hbm, k_hbm, v_hbm, ct_hbm, tau_hbm, msg_hbm,
    q_ref, k_ref, v_ref, ct_ref, tau_ref, states_ref, packed_ref, sums_ref, sems, out_sems,
):
    fetch(
        (
            (tau_hbm, tau_ref),
            (q_hbm, q_ref),
            (k_hbm, k_ref),
            (v_hbm, v_ref),
            (ct_hbm, ct_ref),
        ),
        sems,
    )
    product = q_ref[...].astype(F32) * k_ref[...].astype(F32)
    grad_mixed = ct_ref[...].astype(F32) * v_ref[...].astype(F32)
    rate = by_group_mode(1.0 / tau_ref[...])
    lane = iota((128, 128), 1)
    row = iota((128, 128), 0)
    step = lane.astype(F32)
    decay = jnp.exp(-step * rate)
    left = jnp.float32(L) - step
    decay_end = jnp.exp(-left * rate)
    fwd = dot3(jnp.concatenate([decay_end, left * decay_end], axis=0), product, 1, 1)
    bwd = dot3(jnp.concatenate([decay, step * decay], axis=0), grad_mixed, 1, 1)
    states_ref[:R] = fold_states(fwd[:128])
    states_ref[R:] = fold_states(bwd[:128])
    copies = []

    def send(source, i, rows):
        copies.append(pltpu.make_async_copy(source, msg_hbm.at[plane_slot(i), rows], out_sems.at[len(copies)]))
        copies[-1].start()

    for i in range(NP):
        send(states_ref, i, slice(0, MOMENT_ROW))
    moments = (fold_states(fwd[128:]), fold_states(bwd[128:]))
    for quarter in range(4):
        packed_ref[quarter] = pack_moments(*moments, quarter)
    for i in range(NP):
        send(packed_ref.at[quarter_of(i // 4, i % 4)], i, slice(MOMENT_ROW, SUM_ROW))
    flipped = pick_dot_right(product, ones_where(lane + row == L - 1))
    inside = lane + row >= L - 1
    lags = []
    for g in range(G):
        c = slice(g * M, (g + 1) * M)
        outer = jnp.where(inside, dot3(flipped[c], grad_mixed[c], 0, 0), 0.0)
        lags.append(jnp.sum(pltpu.roll(outer, 1, 1, stride=1, stride_axis=0), axis=0, keepdims=True))
    lags = jnp.concatenate(lags, axis=0)
    lags = jnp.concatenate([lags, lags * step[:G]], axis=0)
    modal = dot3(lags, decay, 1, 1)
    modal = jnp.where(iota((2 * G, G * R), 0) % G == iota((2 * G, G * R), 1) // R, modal, 0.0)
    modal = jnp.concatenate([modal[:G], modal[G:]], axis=1)
    fold = iota((2 * G * R, 128), 0)
    fold = ones_where(fold % R + fold // (G * R) * R == iota((2 * G * R, 128), 1))
    skip = jnp.sum(grad_mixed * product, axis=1, keepdims=True)
    skip = jnp.where(row % M == lane - 2 * R, skip, 0.0)
    pick = ones_where(iota((G, CH), 1) // M == iota((G, CH), 0))
    sums_ref[...] = pick_dot_right(modal, fold) + pick_dot(pick, skip)
    for i in range(NP):
        send(sums_ref, i, slice(SUM_ROW, ROWS))
    for copy in copies:
        copy.wait()


def conv_kernel(
    q_hbm, k_hbm, v_hbm, ct_hbm, skip_hbm, tau_ref, res_ref, fwd_ref, bwd_ref, head_ref, tail_ref, rate_ref, q_ref, k_ref, v_ref, ct_ref, skip_ref, sems
):
    fetch(((q_hbm, q_ref), (k_hbm, k_ref), (v_hbm, v_ref), (ct_hbm, ct_ref), (skip_hbm, skip_ref)), sems)
    product = q_ref[...].astype(F32) * k_ref[...].astype(F32)
    grad_mixed = ct_ref[...].astype(F32) * v_ref[...].astype(F32)
    inv = 1.0 / tau_ref[...]
    rate_ref[...] = by_mode_and_channel(inv)
    rate = by_group_mode(inv)
    gain = by_group_mode(res_ref[...] * jnp.sqrt(2.0 * inv) * (1.0 / math.sqrt(R)))
    lane = iota((128, 128), 1)
    row = iota((128, 128), 0)
    step = lane.astype(F32)
    head = gain * jnp.exp(-step * rate)
    head_ref[...] = head
    tail_ref[...] = gain * jnp.exp(-(jnp.float32(L) - step) * rate)
    taps = jnp.sum(head.reshape(G, R, L), axis=1)
    skip = jnp.sum(jnp.where(lane == row, skip_ref[...], 0.0), axis=1, keepdims=True)
    for g in range(G):
        c = slice(g * M, (g + 1) * M)
        table = pltpu.roll(jnp.broadcast_to(taps[g : g + 1], (L, L)), 0, 1, stride=1, stride_axis=0)
        table = jnp.where(lane >= row, table, 0.0)
        fwd_ref[c] = dot(product[c], table) + skip[c] * product[c]
        bwd_ref[c] = dot(grad_mixed[c], table, 1, 1) + skip[c] * grad_mixed[c]


def plane_index():
    return lax.axis_index("y") * 4 + lax.axis_index("x")


def to_front(state, quarter):
    return pltpu.roll(state, lax.rem(4 - quarter, 4) * SHARE, 1)


def my_quarter():
    return lax.rem(lax.axis_index("y"), 2) * 2 + lax.rem(lax.axis_index("x"), 2)


def plane_kernel(msg_ref, rate_ref, out_ref, carry_ref):
    rate = rate_ref[...]
    me = plane_index()
    quarter = my_quarter()
    span = jnp.float32(L)
    decay = jnp.exp(-span * rate)
    zero = jnp.zeros((R, CH), F32)
    front_decay = to_front(decay, quarter)
    f, g, f1, h0, h1, own_f = zero, zero, zero, zero, zero, zero
    sums = jnp.zeros((G, 128), F32)
    fronts = []
    for i in range(NP):
        at = plane_slot(i)
        own_f = jnp.where(me == i, f, own_f)
        fwd, bwd = msg_ref[at, :R], to_front(msg_ref[at, R : 2 * R], quarter)
        fwd1, bwd1 = unpack_moments(msg_ref[at, MOMENT_ROW:SUM_ROW])
        fronts.append((bwd, bwd1))
        h0 = h0 + g * bwd
        h1 = h1 + g * bwd1 + f1 * bwd
        f1 = front_decay * (f1 + span * g) + fwd1
        g = front_decay * g + to_front(fwd, quarter)
        f = decay * f + fwd
        sums = sums + msg_ref[at, SUM_ROW:]
    b, e, b1, own_b = zero, zero, zero, zero
    for i in reversed(range(NP)):
        bwd, bwd1 = fronts[i]
        own_b = jnp.where(me == i, b, own_b)
        b1 = front_decay * (b1 + span * e) + bwd1
        e = front_decay * e + bwd
        b = decay * b + msg_ref[plane_slot(i), R : 2 * R]
    carry_ref[:R] = own_f
    carry_ref[R : 2 * R] = own_b
    sums = sums + front_sums(h0, h1, quarter)
    sums = jnp.concatenate([pltpu.roll(sums, 3 * SHARE, 1), pltpu.roll(sums, 2 * SHARE, 1)], axis=0)
    place = iota((R, CH), 1) // SHARE
    rest = jnp.where(place == 1, pltpu.roll(f1, SHARE, 1), jnp.where(place == 2, pltpu.roll(b1, 2 * SHARE, 1), sums))
    z = lax.axis_index("z")
    for i in range(NZ):
        above = z < i
        out_ref[z_slot(i), :R] = jnp.where(above, f, b)
        out_ref[z_slot(i), R:] = jnp.where(place == 0, jnp.where(above, e, g), rest)


def final_kernel(msg_ref, tau_ref, res_ref, rate_ref, param_ref):
    inv = 1.0 / tau_ref[...]
    quarter = my_quarter()
    z = lax.axis_index("z")
    span = jnp.float32(L * NP)
    decay = jnp.exp(-span * to_front(rate_ref[...], quarter))
    zero = jnp.zeros((R, CH), F32)
    f, f1, h0, h1 = zero, zero, zero, zero
    total = zero
    for i in range(NZ):
        at = z_slot(i)
        carry = to_front(msg_ref[at, :R], quarter)
        part = msg_ref[at, R:]
        fwd, bwd = jnp.where(i < z, carry, part), jnp.where(i < z, part, carry)
        bwd1 = pltpu.roll(part, 2 * SHARE, 1)
        h0 = h0 + f * bwd
        h1 = h1 + f * bwd1 + f1 * bwd
        f1 = decay * (f1 + span * f) + pltpu.roll(part, 3 * SHARE, 1)
        f = decay * f + fwd
        total = total + part
    whole = front_sums(h0, h1, quarter) + pltpu.roll(total[:G], SHARE, 1)
    scale = 1.0 / math.sqrt(L * NP * NZ * M)
    h0, h1 = whole[:, :R], whole[:, R : 2 * R]
    root = jnp.sqrt(2.0 * inv) * (scale / math.sqrt(R))
    params = jnp.concatenate(
        [h0 * root, res_ref[...] * root * (h1 * inv - 0.5 * h0), jnp.zeros((G, 128 - 2 * R), F32)], axis=1
    )
    group = iota((G, 128), 0) - quarter * (G // 4)
    row = jnp.where(group == 0, params, 0.0)
    for k in range(1, G // 4):
        row = row + jnp.where(group == k, pltpu.roll(params, 2 * R * k, 1), 0.0)
    row = jnp.sum(row, axis=0, keepdims=True)
    for i in range(PEERS):
        param_ref[i] = row


def gather_kernel(part_ref, residue_ref, time_ref):
    rows = part_ref[...].reshape(PEERS, 128)
    columns = jnp.concatenate([rows, jnp.zeros((128 - PEERS, 128), F32)], axis=0).T
    peer = iota((128, 4 * G), 0)
    group = iota((128, 4 * G), 1)
    quarter, core, zh = 3 - peer % 4, peer // 4 % 2, 1 - peer // 8
    first = (zh * 2 + core) * G + quarter * (G // 4)
    out = jnp.zeros((2 * R, 4 * G), F32)
    for k in range(G // 4):
        place = ones_where((group == first + k) & (peer < PEERS)).astype(jnp.bfloat16)
        for part in halves(columns[2 * R * k : 2 * R * (k + 1)]):
            out = out + lax.dot_general(part, place, (((1,), (0,)), ((), ())), preferred_element_type=F32)
    residue_ref[...] = out[:R]
    time_ref[...] = out[R:]


def plane_slot(p):
    return (p - PLANE_FIRST) % NP


def z_slot(z):
    first = jnp.where(lax.axis_index("zh") == 1, Z_FIRST[1], Z_FIRST[0])
    return lax.rem(z + NZ - first, NZ)


def plane_groups():
    return [[(PLANE_FIRST + i) % NP for i in range(NP)]]


def z_groups():
    return [[zh * NZ + (first + i) % NZ for i in range(NZ)] for zh, first in enumerate(Z_FIRST)]


def gather_groups():
    groups = []
    index = lambda zh, z, y, x, core: (((zh * NZ + z) * 4 + y) * 4 + x) * 2 + core
    block = [(zh, core, y, x) for zh in (1, 0) for core in (0, 1) for y in (1, 0) for x in (1, 0)]
    for z in range(NZ):
        planes = {0: z, 1: (z + 4) % NZ}
        for top in (0, 2):
            for left in (0, 2):
                groups.append([index(zh, planes[zh], top + y, left + x, core) for zh, core, y, x in block])
    return groups


def output_kernel(
    q_hbm, k_hbm, v_hbm, ct_hbm, fwd_ref, bwd_ref, head_ref, tail_ref, msg_ref, plane_ref, rate_ref,
    out_ref, gq_ref, gk_ref, gv_ref, skip_ref, q_ref, k_ref, v_ref, ct_ref, sems,
):
    fetch(((q_hbm, q_ref), (k_hbm, k_ref), (v_hbm, v_ref), (ct_hbm, ct_ref)), sems)
    rate = rate_ref[...]
    z = lax.axis_index("z")
    me = plane_index().astype(F32)
    decay = jnp.exp(-jnp.float32(L * NP) * rate)
    own_f = jnp.zeros((R, CH), F32)
    own_b = own_f
    sums = jnp.zeros((G, 128), F32)
    for i in range(NZ):
        own_f = jnp.where(i < z, decay * own_f + msg_ref[z_slot(i), :R], own_f)
        sums = sums + msg_ref[z_slot(i), R + G :]
    for i in reversed(range(NZ)):
        own_b = jnp.where(i > z, decay * own_b + msg_ref[z_slot(i), :R], own_b)
    own_f = plane_ref[:R] + jnp.exp(-(L * me) * rate) * own_f
    own_b = plane_ref[R : 2 * R] + jnp.exp(-(L * (NP - 1 - me)) * rate) * own_b
    lane = iota((128, 128), 1)
    row = iota((128, 128), 0)
    spread = dot(sums, ones_where((row - 3 * SHARE == lane % M) & (row >= 3 * SHARE) & (row < 3 * SHARE + M)))
    spread = jnp.where(iota((G, CH), 1) // M == iota((G, CH), 0), spread, 0.0)
    skip_ref[...] = jnp.sum(spread, axis=0, keepdims=True) * (1.0 / math.sqrt(L * NP * NZ))
    mixed = fwd_ref[...] + dot3(spread_states(own_f), head_ref[...], 0, 0)
    grad_product = bwd_ref[...] + dot3(spread_states(own_b), tail_ref[...], 0, 0)
    out_ref[...] = (v_ref[...].astype(F32) * mixed).astype(jnp.bfloat16)
    gv_ref[...] = (ct_ref[...].astype(F32) * mixed).astype(jnp.bfloat16)
    gq_ref[...] = (grad_product * k_ref[...].astype(F32)).astype(jnp.bfloat16)
    gk_ref[...] = (grad_product * q_ref[...].astype(F32)).astype(jnp.bfloat16)


def shape(*dims, dtype=F32):
    return jax.ShapeDtypeStruct(dims, dtype)


def call(kernel, outs, flops, name, vmem=32 * 1024 * 1024, **options):
    return pl.pallas_call(
        kernel,
        out_shape=outs,
        name=name,
        cost_estimate=pl.CostEstimate(flops=flops, bytes_accessed=500_000, transcendentals=0),
        compiler_params=pltpu.CompilerParams(vmem_limit_bytes=vmem),
        **options,
    )


def per_device(queries, key_inputs, value_inputs, skip_gain, residue, timescale, cotangent):
    arrays = (queries, key_inputs, value_inputs, cotangent)
    hbm = pl.BlockSpec(memory_space=pltpu.HBM)
    local = pl.BlockSpec(memory_space=pltpu.VMEM)
    blocks = [pltpu.VMEM((CH, L), jnp.bfloat16)] * 4
    message = call(
        local_kernel,
        shape(NP, ROWS, 128),
        10**8,
        "local_states",
        vmem=60 * 1024 * 1024,
        in_specs=[hbm] * 5,
        out_specs=hbm,
        scratch_shapes=[
            *blocks,
            pltpu.VMEM((G, R), F32),
            pltpu.VMEM((2 * R, CH), F32),
            pltpu.VMEM((4, 8, CH), F32),
            pltpu.VMEM((G, CH), F32),
            pltpu.SemaphoreType.DMA((5,)),
            pltpu.SemaphoreType.DMA((3 * NP,)),
        ],
    )(*arrays, timescale)
    plane_states = lax.all_to_all(message, ("y", "x"), 0, 0, axis_index_groups=plane_groups())
    *tables, rate = call(
        conv_kernel,
        (*(shape(128, 128),) * 4, shape(R, CH)),
        10**8,
        "local_conv",
        in_specs=[hbm] * 5 + [local] * 2,
        scratch_shapes=[*blocks, pltpu.VMEM((1, CH), F32), pltpu.SemaphoreType.DMA((5,))],
    )(*arrays, skip_gain.reshape(1, CH), timescale, residue)
    totals, plane_carry = call(plane_kernel, (shape(NZ, Z_ROWS, 128), shape(2 * R, CH)), 10**7, "plane_scan")(
        plane_states, rate
    )
    z_states = lax.all_to_all(totals, ("zh", "z"), 0, 0, axis_index_groups=z_groups())
    params = call(final_kernel, shape(PEERS, 1, 128), 10**7, "z_scan")(z_states, timescale, residue, rate)
    params = lax.all_to_all(params, ("zh", "z", "y", "x", "core"), 0, 0, axis_index_groups=gather_groups())
    output, grad_queries, grad_keys, grad_values, grad_skip = call(
        output_kernel,
        (*(shape(CH, L, dtype=jnp.bfloat16),) * 4, shape(1, CH)),
        10**8,
        "outputs",
        in_specs=[hbm] * 4 + [local] * 7,
        scratch_shapes=[*blocks, pltpu.SemaphoreType.DMA((4,))],
    )(*arrays, *tables, z_states, plane_carry, rate)
    grad_residue, grad_time = call(gather_kernel, (shape(R, 4 * G),) * 2, 10**6, "gather")(params)
    return (
        output,
        grad_queries,
        grad_keys,
        grad_values,
        grad_skip.reshape(CH),
        grad_residue.T,
        grad_time.T,
    )


def solution(mesh):
    grid = Mesh(mesh.devices.reshape(NZ, 4, 4, 2, 2), ("z", "y", "x", "zh", "core"))
    seq = ("z", "y", "x")
    ch = ("zh", "core")
    return jax.shard_map(
        per_device,
        mesh=grid,
        in_specs=(P(ch, seq), P(ch, seq), P(ch, seq), P(ch), P(ch, None), P(ch, None), P(ch, seq)),
        out_specs=(P(ch, seq), P(ch, seq), P(ch, seq), P(ch, seq), P(ch), P(), P()),
        check_vma=False,
    )
```

```python
import math

import jax
import jax.numpy as jnp
from jax import lax
from jax.experimental import pallas as pl
from jax.experimental.pallas import tpu as pltpu
from jax.sharding import Mesh, PartitionSpec as P

F32 = jnp.float32
HI = lax.Precision.HIGHEST
L = 128
CH = 128
G = 8
R = 16
M = 16
MOMENT_ROW = 2 * R
SUM_ROW = MOMENT_ROW + R // 2
ROWS = SUM_ROW + G
NP = 16
NZ = 8
SHARE = CH // 4
Z_ROWS = 2 * R
PEERS = 16
PLANE_FIRST = 15
Z_ORDER = ((7, 0, 6, 1, 5, 2, 4, 3), (3, 4, 2, 5, 1, 6, 0, 7))
Z_PARTNER = (7, 5, 4, 6, 0, 1, 2, 3)


def dot(a, b, ca=1, cb=0):
    return lax.dot_general(a, b, (((ca,), (cb,)), ((), ())), precision=HI, preferred_element_type=F32)


def halves(value):
    high = value.astype(jnp.bfloat16)
    return high, (value - high.astype(F32)).astype(jnp.bfloat16)


def dot3(a, b, ca=1, cb=0):
    (a_high, a_low), (b_high, b_low) = halves(a), halves(b)
    left = jnp.concatenate([a_high, a_high, a_low], axis=ca)
    right = jnp.concatenate([b_high, b_low, b_high], axis=cb)
    return lax.dot_general(left, right, (((ca,), (cb,)), ((), ())), preferred_element_type=F32)


def pick_dot(pick, b, ca=1, cb=0):
    pick = pick.astype(jnp.bfloat16)
    left = jnp.concatenate([pick, pick], axis=ca)
    right = jnp.concatenate(halves(b), axis=cb)
    return lax.dot_general(left, right, (((ca,), (cb,)), ((), ())), preferred_element_type=F32)


def pick_dot_right(a, pick):
    pick = pick.astype(jnp.bfloat16)
    left = jnp.concatenate(halves(a), axis=1)
    right = jnp.concatenate([pick, pick], axis=0)
    return lax.dot_general(left, right, (((1,), (0,)), ((), ())), preferred_element_type=F32)


def iota(shape, axis):
    return lax.broadcasted_iota(jnp.int32, shape, axis)


def ones_where(cond):
    return jnp.where(cond, jnp.float32(1), jnp.float32(0))


def by_mode_and_channel(table):
    pick = ones_where(iota((G, CH), 1) // M == iota((G, CH), 0))
    return dot(table, pick, 0, 0)


def by_group_mode(table):
    rows = jnp.concatenate([jnp.broadcast_to(table[g : g + 1], (R, R)) for g in range(G)], axis=0)
    rows = jnp.where(iota((G * R, R), 0) % R == iota((G * R, R), 1), rows, 0.0)
    return jnp.sum(rows, axis=1, keepdims=True)


def same_group():
    return iota((128, 128), 0) // M == iota((128, 128), 1) // M


def fold_states(full):
    own = jnp.where(same_group(), full, 0.0)
    return jnp.sum(own.reshape(G, R, CH), axis=0)


def spread_states(state):
    return jnp.where(same_group(), jnp.concatenate([state] * G, axis=0), 0.0)


def front_sums(h0, h1, quarter):
    lane = iota((G, CH), 1)
    pick = ones_where((lane // M + quarter * (SHARE // M) == iota((G, CH), 0)) & (lane < SHARE))
    front = iota((R, CH), 1) < SHARE
    rows = [jnp.where(front, h0, 0.0), jnp.where(front, h1, 0.0), jnp.zeros((CH - 2 * R, CH), F32)]
    return pick_dot(pick, jnp.concatenate(rows, axis=0), 1, 1)


def fetch(pairs, sems):
    copies = [pltpu.make_async_copy(src, dst, sems.at[i]) for i, (src, dst) in enumerate(pairs)]
    for copy in copies:
        copy.start()
    for copy in copies:
        copy.wait()


def quarter_of(y, x):
    return y % 2 * 2 + x % 2


def pack_moments(a, b, quarter):
    packed = jnp.zeros((8, CH), F32)
    for k, piece in enumerate((a[:8], a[8:], b[:8], b[8:])):
        packed = jnp.where(iota((8, CH), 1) // SHARE == k, pltpu.roll(piece, (k - quarter) % 4 * SHARE, 1), packed)
    return packed


def unpack_moments(packed):
    moved = [packed] + [pltpu.roll(packed, CH - k * SHARE, 1) for k in range(1, 4)]
    return jnp.concatenate(moved[:2], axis=0), jnp.concatenate(moved[2:], axis=0)


def local_kernel(
    q_hbm, k_hbm, v_hbm, ct_hbm, tau_hbm, msg_hbm,
    q_ref, k_ref, v_ref, ct_ref, tau_ref, states_ref, packed_ref, sums_ref, sems, out_sems,
):
    fetch(
        (
            (tau_hbm, tau_ref),
            (q_hbm, q_ref),
            (k_hbm, k_ref),
            (v_hbm, v_ref),
            (ct_hbm, ct_ref),
        ),
        sems,
    )
    product = q_ref[...].astype(F32) * k_ref[...].astype(F32)
    grad_mixed = ct_ref[...].astype(F32) * v_ref[...].astype(F32)
    rate = by_group_mode(1.0 / tau_ref[...])
    lane = iota((128, 128), 1)
    row = iota((128, 128), 0)
    step = lane.astype(F32)
    decay = jnp.exp(-step * rate)
    left = jnp.float32(L) - step
    decay_end = jnp.exp(-left * rate)
    fwd = dot3(jnp.concatenate([decay_end, left * decay_end], axis=0), product, 1, 1)
    bwd = dot3(jnp.concatenate([decay, step * decay], axis=0), grad_mixed, 1, 1)
    states_ref[:R] = fold_states(fwd[:128])
    states_ref[R:] = fold_states(bwd[:128])
    copies = []

    def send(source, i, rows):
        copies.append(pltpu.make_async_copy(source, msg_hbm.at[plane_slot(i), rows], out_sems.at[len(copies)]))
        copies[-1].start()

    for i in range(NP):
        send(states_ref, i, slice(0, MOMENT_ROW))
    moments = (fold_states(fwd[128:]), fold_states(bwd[128:]))
    for quarter in range(4):
        packed_ref[quarter] = pack_moments(*moments, quarter)
    for i in range(NP):
        send(packed_ref.at[quarter_of(i // 4, i % 4)], i, slice(MOMENT_ROW, SUM_ROW))
    flipped = pick_dot_right(product, ones_where(lane + row == L - 1))
    inside = lane + row >= L - 1
    lags = []
    for g in range(G):
        c = slice(g * M, (g + 1) * M)
        outer = jnp.where(inside, dot3(flipped[c], grad_mixed[c], 0, 0), 0.0)
        lags.append(jnp.sum(pltpu.roll(outer, 1, 1, stride=1, stride_axis=0), axis=0, keepdims=True))
    lags = jnp.concatenate(lags, axis=0)
    lags = jnp.concatenate([lags, lags * step[:G]], axis=0)
    modal = dot3(lags, decay, 1, 1)
    modal = jnp.where(iota((2 * G, G * R), 0) % G == iota((2 * G, G * R), 1) // R, modal, 0.0)
    modal = jnp.concatenate([modal[:G], modal[G:]], axis=1)
    fold = iota((2 * G * R, 128), 0)
    fold = ones_where(fold % R + fold // (G * R) * R == iota((2 * G * R, 128), 1))
    skip = jnp.sum(grad_mixed * product, axis=1, keepdims=True)
    skip = jnp.where(row % M == lane - 2 * R, skip, 0.0)
    pick = ones_where(iota((G, CH), 1) // M == iota((G, CH), 0))
    sums_ref[...] = pick_dot_right(modal, fold) + pick_dot(pick, skip)
    for i in range(NP):
        send(sums_ref, i, slice(SUM_ROW, ROWS))
    for copy in copies:
        copy.wait()


def conv_kernel(
    q_hbm, k_hbm, v_hbm, ct_hbm, skip_hbm, tau_ref, res_ref, fwd_ref, bwd_ref, head_ref, tail_ref, rate_ref, q_ref, k_ref, v_ref, ct_ref, skip_ref, sems
):
    fetch(((q_hbm, q_ref), (k_hbm, k_ref), (v_hbm, v_ref), (ct_hbm, ct_ref), (skip_hbm, skip_ref)), sems)
    product = q_ref[...].astype(F32) * k_ref[...].astype(F32)
    grad_mixed = ct_ref[...].astype(F32) * v_ref[...].astype(F32)
    inv = 1.0 / tau_ref[...]
    rate_ref[...] = by_mode_and_channel(inv)
    rate = by_group_mode(inv)
    gain = by_group_mode(res_ref[...] * jnp.sqrt(2.0 * inv) * (1.0 / math.sqrt(R)))
    lane = iota((128, 128), 1)
    row = iota((128, 128), 0)
    step = lane.astype(F32)
    head = gain * jnp.exp(-step * rate)
    head_ref[...] = head
    tail_ref[...] = gain * jnp.exp(-(jnp.float32(L) - step) * rate)
    taps = jnp.sum(head.reshape(G, R, L), axis=1)
    skip = jnp.sum(jnp.where(lane == row, skip_ref[...], 0.0), axis=1, keepdims=True)
    for g in range(G):
        c = slice(g * M, (g + 1) * M)
        table = pltpu.roll(jnp.broadcast_to(taps[g : g + 1], (L, L)), 0, 1, stride=1, stride_axis=0)
        table = jnp.where(lane >= row, table, 0.0)
        fwd_ref[c] = dot(product[c], table) + skip[c] * product[c]
        bwd_ref[c] = dot(grad_mixed[c], table, 1, 1) + skip[c] * grad_mixed[c]


def plane_index():
    return lax.axis_index("y") * 4 + lax.axis_index("x")


def to_front(state, quarter):
    return pltpu.roll(state, lax.rem(4 - quarter, 4) * SHARE, 1)


def my_quarter():
    return lax.rem(lax.axis_index("y"), 2) * 2 + lax.rem(lax.axis_index("x"), 2)


def plane_kernel(msg_ref, rate_ref, out_ref, carry_ref):
    rate = rate_ref[...]
    me = plane_index()
    quarter = my_quarter()
    span = jnp.float32(L)
    decay = jnp.exp(-span * rate)
    zero = jnp.zeros((R, CH), F32)
    front_decay = to_front(decay, quarter)
    f, g, f1, h0, h1, own_f = zero, zero, zero, zero, zero, zero
    sums = jnp.zeros((G, 128), F32)
    fronts = []
    for i in range(NP):
        at = plane_slot(i)
        own_f = jnp.where(me == i, f, own_f)
        fwd, bwd = msg_ref[at, :R], to_front(msg_ref[at, R : 2 * R], quarter)
        fwd1, bwd1 = unpack_moments(msg_ref[at, MOMENT_ROW:SUM_ROW])
        fronts.append((bwd, bwd1))
        h0 = h0 + g * bwd
        h1 = h1 + g * bwd1 + f1 * bwd
        f1 = front_decay * (f1 + span * g) + fwd1
        g = front_decay * g + to_front(fwd, quarter)
        f = decay * f + fwd
        sums = sums + msg_ref[at, SUM_ROW:]
    b, e, b1, own_b = zero, zero, zero, zero
    for i in reversed(range(NP)):
        bwd, bwd1 = fronts[i]
        own_b = jnp.where(me == i, b, own_b)
        b1 = front_decay * (b1 + span * e) + bwd1
        e = front_decay * e + bwd
        b = decay * b + msg_ref[plane_slot(i), R : 2 * R]
    carry_ref[:R] = own_f
    carry_ref[R : 2 * R] = own_b
    sums = sums + front_sums(h0, h1, quarter)
    sums = jnp.concatenate([pltpu.roll(sums, 3 * SHARE, 1), pltpu.roll(sums, 2 * SHARE, 1)], axis=0)
    place = iota((R, CH), 1) // SHARE
    rest = jnp.where(place == 1, pltpu.roll(f1, SHARE, 1), jnp.where(place == 2, pltpu.roll(b1, 2 * SHARE, 1), sums))
    z = lax.axis_index("z")
    for i in range(NZ):
        above = z < i
        out_ref[z_slot(i), :R] = jnp.where(above, f, b)
        out_ref[z_slot(i), R:] = jnp.where(place == 0, jnp.where(above, e, g), rest)


def final_kernel(msg_ref, tau_ref, res_ref, rate_ref, param_ref):
    inv = 1.0 / tau_ref[...]
    quarter = my_quarter()
    z = lax.axis_index("z")
    span = jnp.float32(L * NP)
    decay = jnp.exp(-span * to_front(rate_ref[...], quarter))
    zero = jnp.zeros((R, CH), F32)
    f, f1, h0, h1 = zero, zero, zero, zero
    total = zero
    for i in range(NZ):
        at = z_slot(i)
        carry = to_front(msg_ref[at, :R], quarter)
        part = msg_ref[at, R:]
        fwd, bwd = jnp.where(i < z, carry, part), jnp.where(i < z, part, carry)
        bwd1 = pltpu.roll(part, 2 * SHARE, 1)
        h0 = h0 + f * bwd
        h1 = h1 + f * bwd1 + f1 * bwd
        f1 = decay * (f1 + span * f) + pltpu.roll(part, 3 * SHARE, 1)
        f = decay * f + fwd
        total = total + part
    whole = front_sums(h0, h1, quarter) + pltpu.roll(total[:G], SHARE, 1)
    scale = 1.0 / math.sqrt(L * NP * NZ * M)
    h0, h1 = whole[:, :R], whole[:, R : 2 * R]
    root = jnp.sqrt(2.0 * inv) * (scale / math.sqrt(R))
    params = jnp.concatenate(
        [h0 * root, res_ref[...] * root * (h1 * inv - 0.5 * h0), jnp.zeros((G, 128 - 2 * R), F32)], axis=1
    )
    group = iota((G, 128), 0) - quarter * (G // 4)
    row = jnp.where(group == 0, params, 0.0)
    for k in range(1, G // 4):
        row = row + jnp.where(group == k, pltpu.roll(params, 2 * R * k, 1), 0.0)
    row = jnp.sum(row, axis=0, keepdims=True)
    for i in range(PEERS):
        param_ref[i] = row


def gather_kernel(part_ref, residue_ref, time_ref):
    rows = part_ref[...].reshape(PEERS, 128)
    columns = jnp.concatenate([rows, jnp.zeros((128 - PEERS, 128), F32)], axis=0).T
    peer = iota((128, 4 * G), 0)
    group = iota((128, 4 * G), 1)
    quarter, core, zh = 3 - peer % 4, peer // 4 % 2, 1 - peer // 8
    first = (zh * 2 + core) * G + quarter * (G // 4)
    out = jnp.zeros((2 * R, 4 * G), F32)
    for k in range(G // 4):
        place = ones_where((group == first + k) & (peer < PEERS)).astype(jnp.bfloat16)
        for part in halves(columns[2 * R * k : 2 * R * (k + 1)]):
            out = out + lax.dot_general(part, place, (((1,), (0,)), ((), ())), preferred_element_type=F32)
    residue_ref[...] = out[:R]
    time_ref[...] = out[R:]


def plane_slot(p):
    return (p - PLANE_FIRST) % NP


def z_slot(z):
    return jnp.where(lax.axis_index("zh") == 1, Z_ORDER[1].index(z), Z_ORDER[0].index(z))


def plane_groups():
    return [[(PLANE_FIRST + i) % NP for i in range(NP)]]


def z_groups():
    return [[zh * NZ + z for z in order] for zh, order in enumerate(Z_ORDER)]


def gather_groups():
    groups = []
    index = lambda zh, z, y, x, core: (((zh * NZ + z) * 4 + y) * 4 + x) * 2 + core
    block = [(zh, core, y, x) for zh in (1, 0) for core in (0, 1) for y in (1, 0) for x in (1, 0)]
    for z in range(NZ):
        planes = {0: z, 1: Z_PARTNER[z]}
        for top in (0, 2):
            for left in (0, 2):
                groups.append([index(zh, planes[zh], top + y, left + x, core) for zh, core, y, x in block])
    return groups


def output_kernel(
    q_hbm, k_hbm, v_hbm, ct_hbm, fwd_ref, bwd_ref, head_ref, tail_ref, msg_ref, plane_ref, rate_ref,
    out_ref, gq_ref, gk_ref, gv_ref, skip_ref, q_ref, k_ref, v_ref, ct_ref, sems,
):
    fetch(((q_hbm, q_ref), (k_hbm, k_ref), (v_hbm, v_ref), (ct_hbm, ct_ref)), sems)
    rate = rate_ref[...]
    z = lax.axis_index("z")
    me = plane_index().astype(F32)
    decay = jnp.exp(-jnp.float32(L * NP) * rate)
    own_f = jnp.zeros((R, CH), F32)
    own_b = own_f
    sums = jnp.zeros((G, 128), F32)
    for i in range(NZ):
        own_f = jnp.where(i < z, decay * own_f + msg_ref[z_slot(i), :R], own_f)
        sums = sums + msg_ref[z_slot(i), R + G :]
    for i in reversed(range(NZ)):
        own_b = jnp.where(i > z, decay * own_b + msg_ref[z_slot(i), :R], own_b)
    own_f = plane_ref[:R] + jnp.exp(-(L * me) * rate) * own_f
    own_b = plane_ref[R : 2 * R] + jnp.exp(-(L * (NP - 1 - me)) * rate) * own_b
    lane = iota((128, 128), 1)
    row = iota((128, 128), 0)
    spread = dot(sums, ones_where((row - 3 * SHARE == lane % M) & (row >= 3 * SHARE) & (row < 3 * SHARE + M)))
    spread = jnp.where(iota((G, CH), 1) // M == iota((G, CH), 0), spread, 0.0)
    skip_ref[...] = jnp.sum(spread, axis=0, keepdims=True) * (1.0 / math.sqrt(L * NP * NZ))
    mixed = fwd_ref[...] + dot3(spread_states(own_f), head_ref[...], 0, 0)
    grad_product = bwd_ref[...] + dot3(spread_states(own_b), tail_ref[...], 0, 0)
    out_ref[...] = (v_ref[...].astype(F32) * mixed).astype(jnp.bfloat16)
    gv_ref[...] = (ct_ref[...].astype(F32) * mixed).astype(jnp.bfloat16)
    gq_ref[...] = (grad_product * k_ref[...].astype(F32)).astype(jnp.bfloat16)
    gk_ref[...] = (grad_product * q_ref[...].astype(F32)).astype(jnp.bfloat16)


def shape(*dims, dtype=F32):
    return jax.ShapeDtypeStruct(dims, dtype)


def call(kernel, outs, flops, name, vmem=32 * 1024 * 1024, **options):
    return pl.pallas_call(
        kernel,
        out_shape=outs,
        name=name,
        cost_estimate=pl.CostEstimate(flops=flops, bytes_accessed=500_000, transcendentals=0),
        compiler_params=pltpu.CompilerParams(vmem_limit_bytes=vmem),
        **options,
    )


def per_device(queries, key_inputs, value_inputs, skip_gain, residue, timescale, cotangent):
    arrays = (queries, key_inputs, value_inputs, cotangent)
    hbm = pl.BlockSpec(memory_space=pltpu.HBM)
    local = pl.BlockSpec(memory_space=pltpu.VMEM)
    blocks = [pltpu.VMEM((CH, L), jnp.bfloat16)] * 4
    message = call(
        local_kernel,
        shape(NP, ROWS, 128),
        10**8,
        "local_states",
        vmem=60 * 1024 * 1024,
        in_specs=[hbm] * 5,
        out_specs=hbm,
        scratch_shapes=[
            *blocks,
            pltpu.VMEM((G, R), F32),
            pltpu.VMEM((2 * R, CH), F32),
            pltpu.VMEM((4, 8, CH), F32),
            pltpu.VMEM((G, CH), F32),
            pltpu.SemaphoreType.DMA((5,)),
            pltpu.SemaphoreType.DMA((3 * NP,)),
        ],
    )(*arrays, timescale)
    plane_states = lax.all_to_all(message, ("y", "x"), 0, 0, axis_index_groups=plane_groups())
    *tables, rate = call(
        conv_kernel,
        (*(shape(128, 128),) * 4, shape(R, CH)),
        10**8,
        "local_conv",
        in_specs=[hbm] * 5 + [local] * 2,
        scratch_shapes=[*blocks, pltpu.VMEM((1, CH), F32), pltpu.SemaphoreType.DMA((5,))],
    )(*arrays, skip_gain.reshape(1, CH), timescale, residue)
    totals, plane_carry = call(plane_kernel, (shape(NZ, Z_ROWS, 128), shape(2 * R, CH)), 10**7, "plane_scan")(
        plane_states, rate
    )
    z_states = lax.all_to_all(totals, ("zh", "z"), 0, 0, axis_index_groups=z_groups())
    params = call(final_kernel, shape(PEERS, 1, 128), 10**7, "z_scan")(z_states, timescale, residue, rate)
    params = lax.all_to_all(params, ("zh", "z", "y", "x", "core"), 0, 0, axis_index_groups=gather_groups())
    output, grad_queries, grad_keys, grad_values, grad_skip = call(
        output_kernel,
        (*(shape(CH, L, dtype=jnp.bfloat16),) * 4, shape(1, CH)),
        10**8,
        "outputs",
        in_specs=[hbm] * 4 + [local] * 7,
        scratch_shapes=[*blocks, pltpu.SemaphoreType.DMA((4,))],
    )(*arrays, *tables, z_states, plane_carry, rate)
    grad_residue, grad_time = call(gather_kernel, (shape(R, 4 * G),) * 2, 10**6, "gather")(params)
    return (
        output,
        grad_queries,
        grad_keys,
        grad_values,
        grad_skip.reshape(CH),
        grad_residue.T,
        grad_time.T,
    )


def solution(mesh):
    grid = Mesh(mesh.devices.reshape(NZ, 4, 4, 2, 2), ("z", "y", "x", "zh", "core"))
    seq = ("z", "y", "x")
    ch = ("zh", "core")
    return jax.shard_map(
        per_device,
        mesh=grid,
        in_specs=(P(ch, seq), P(ch, seq), P(ch, seq), P(ch), P(ch, None), P(ch, None), P(ch, seq)),
        out_specs=(P(ch, seq), P(ch, seq), P(ch, seq), P(ch, seq), P(ch), P(), P()),
        check_vma=False,
    )
```

```python
import math

import jax
import jax.numpy as jnp
from jax import lax
from jax.experimental import pallas as pl
from jax.experimental.pallas import tpu as pltpu
from jax.sharding import Mesh, PartitionSpec as P

F32 = jnp.float32
HI = lax.Precision.HIGHEST
L = 128
CH = 128
G = 8
R = 16
M = 16
MOMENT_ROW = 2 * R
SUM_ROW = MOMENT_ROW + R // 2
ROWS = SUM_ROW + G
NP = 16
NZ = 8
SHARE = CH // 4
Z_ROWS = 2 * R
PEERS = 16
PLANE_ORDER = (15, 14, 11, 13, 10, 7, 12, 9, 6, 3, 8, 5, 2, 4, 1, 0)
Z_ORDER = ((7, 0, 6, 1, 5, 2, 4, 3), (3, 4, 2, 5, 1, 6, 0, 7))
Z_PARTNER = (6, 7, 5, 0, 1, 2, 3, 4)


def dot(a, b, ca=1, cb=0):
    return lax.dot_general(a, b, (((ca,), (cb,)), ((), ())), precision=HI, preferred_element_type=F32)


def halves(value):
    high = value.astype(jnp.bfloat16)
    return high, (value - high.astype(F32)).astype(jnp.bfloat16)


def dot3(a, b, ca=1, cb=0):
    (a_high, a_low), (b_high, b_low) = halves(a), halves(b)
    left = jnp.concatenate([a_high, a_high, a_low], axis=ca)
    right = jnp.concatenate([b_high, b_low, b_high], axis=cb)
    return lax.dot_general(left, right, (((ca,), (cb,)), ((), ())), preferred_element_type=F32)


def pick_dot(pick, b, ca=1, cb=0):
    pick = pick.astype(jnp.bfloat16)
    left = jnp.concatenate([pick, pick], axis=ca)
    right = jnp.concatenate(halves(b), axis=cb)
    return lax.dot_general(left, right, (((ca,), (cb,)), ((), ())), preferred_element_type=F32)


def pick_dot_right(a, pick):
    pick = pick.astype(jnp.bfloat16)
    left = jnp.concatenate(halves(a), axis=1)
    right = jnp.concatenate([pick, pick], axis=0)
    return lax.dot_general(left, right, (((1,), (0,)), ((), ())), preferred_element_type=F32)


def iota(shape, axis):
    return lax.broadcasted_iota(jnp.int32, shape, axis)


def ones_where(cond):
    return jnp.where(cond, jnp.float32(1), jnp.float32(0))


def by_mode_and_channel(table):
    pick = ones_where(iota((G, CH), 1) // M == iota((G, CH), 0))
    return dot(table, pick, 0, 0)


def by_group_mode(table):
    rows = jnp.concatenate([jnp.broadcast_to(table[g : g + 1], (R, R)) for g in range(G)], axis=0)
    rows = jnp.where(iota((G * R, R), 0) % R == iota((G * R, R), 1), rows, 0.0)
    return jnp.sum(rows, axis=1, keepdims=True)


def same_group():
    return iota((128, 128), 0) // M == iota((128, 128), 1) // M


def fold_states(full):
    own = jnp.where(same_group(), full, 0.0)
    return jnp.sum(own.reshape(G, R, CH), axis=0)


def spread_states(state):
    return jnp.where(same_group(), jnp.concatenate([state] * G, axis=0), 0.0)


def front_sums(h0, h1, quarter):
    lane = iota((G, CH), 1)
    pick = ones_where((lane // M + quarter * (SHARE // M) == iota((G, CH), 0)) & (lane < SHARE))
    front = iota((R, CH), 1) < SHARE
    rows = [jnp.where(front, h0, 0.0), jnp.where(front, h1, 0.0), jnp.zeros((CH - 2 * R, CH), F32)]
    return pick_dot(pick, jnp.concatenate(rows, axis=0), 1, 1)


def fetch(pairs, sems):
    copies = [pltpu.make_async_copy(src, dst, sems.at[i]) for i, (src, dst) in enumerate(pairs)]
    for copy in copies:
        copy.start()
    for copy in copies:
        copy.wait()


def quarter_of(y, x):
    return y % 2 * 2 + x % 2


def pack_moments(a, b, quarter):
    packed = jnp.zeros((8, CH), F32)
    for k, piece in enumerate((a[:8], a[8:], b[:8], b[8:])):
        packed = jnp.where(iota((8, CH), 1) // SHARE == k, pltpu.roll(piece, (k - quarter) % 4 * SHARE, 1), packed)
    return packed


def unpack_moments(packed):
    moved = [packed] + [pltpu.roll(packed, CH - k * SHARE, 1) for k in range(1, 4)]
    return jnp.concatenate(moved[:2], axis=0), jnp.concatenate(moved[2:], axis=0)


def local_kernel(
    q_hbm, k_hbm, v_hbm, ct_hbm, tau_hbm, msg_hbm,
    q_ref, k_ref, v_ref, ct_ref, tau_ref, states_ref, packed_ref, sums_ref, sems, out_sems,
):
    pairs = ((tau_hbm, tau_ref), (q_hbm, q_ref), (k_hbm, k_ref), (v_hbm, v_ref), (ct_hbm, ct_ref))
    fetches = [pltpu.make_async_copy(source, target, sems.at[i]) for i, (source, target) in enumerate(pairs)]
    for copy in fetches:
        copy.start()
    fetches[0].wait()
    rate = by_group_mode(1.0 / tau_ref[...])
    lane = iota((128, 128), 1)
    row = iota((128, 128), 0)
    step = lane.astype(F32)
    decay = jnp.exp(-step * rate)
    left = jnp.float32(L) - step
    decay_end = jnp.exp(-left * rate)
    for copy in fetches[1:]:
        copy.wait()
    product = q_ref[...].astype(F32) * k_ref[...].astype(F32)
    grad_mixed = ct_ref[...].astype(F32) * v_ref[...].astype(F32)
    fwd = dot3(jnp.concatenate([decay_end, left * decay_end], axis=0), product, 1, 1)
    bwd = dot3(jnp.concatenate([decay, step * decay], axis=0), grad_mixed, 1, 1)
    states_ref[:R] = fold_states(fwd[:128])
    states_ref[R:] = fold_states(bwd[:128])
    copies = []

    def send(source, i, rows):
        copies.append(pltpu.make_async_copy(source, msg_hbm.at[plane_slot(i), rows], out_sems.at[len(copies)]))
        copies[-1].start()

    for i in range(NP):
        send(states_ref, i, slice(0, MOMENT_ROW))
    moments = (fold_states(fwd[128:]), fold_states(bwd[128:]))
    for quarter in range(4):
        packed_ref[quarter] = pack_moments(*moments, quarter)
    for i in range(NP):
        send(packed_ref.at[quarter_of(i // 4, i % 4)], i, slice(MOMENT_ROW, SUM_ROW))
    flipped = pick_dot_right(product, ones_where(lane + row == L - 1))
    inside = lane + row >= L - 1
    lags = []
    for g in range(G):
        c = slice(g * M, (g + 1) * M)
        outer = jnp.where(inside, dot3(flipped[c], grad_mixed[c], 0, 0), 0.0)
        lags.append(jnp.sum(pltpu.roll(outer, 1, 1, stride=1, stride_axis=0), axis=0, keepdims=True))
    lags = jnp.concatenate(lags, axis=0)
    lags = jnp.concatenate([lags, lags * step[:G]], axis=0)
    modal = dot3(lags, decay, 1, 1)
    modal = jnp.where(iota((2 * G, G * R), 0) % G == iota((2 * G, G * R), 1) // R, modal, 0.0)
    modal = jnp.concatenate([modal[:G], modal[G:]], axis=1)
    fold = iota((2 * G * R, 128), 0)
    fold = ones_where(fold % R + fold // (G * R) * R == iota((2 * G * R, 128), 1))
    skip = jnp.sum(grad_mixed * product, axis=1, keepdims=True)
    skip = jnp.where(row % M == lane - 2 * R, skip, 0.0)
    pick = ones_where(iota((G, CH), 1) // M == iota((G, CH), 0))
    sums_ref[...] = pick_dot_right(modal, fold) + pick_dot(pick, skip)
    for i in range(NP):
        send(sums_ref, i, slice(SUM_ROW, ROWS))
    for copy in copies:
        copy.wait()


def conv_kernel(
    q_hbm, k_hbm, v_hbm, ct_hbm, skip_hbm, tau_ref, res_ref, fwd_ref, bwd_ref, head_ref, tail_ref, rate_ref, factor_ref, q_ref, k_ref, v_ref, ct_ref, skip_ref, sems
):
    fetch(((q_hbm, q_ref), (k_hbm, k_ref), (v_hbm, v_ref), (ct_hbm, ct_ref), (skip_hbm, skip_ref)), sems)
    product = q_ref[...].astype(F32) * k_ref[...].astype(F32)
    grad_mixed = ct_ref[...].astype(F32) * v_ref[...].astype(F32)
    inv = 1.0 / tau_ref[...]
    rate_ref[...] = by_mode_and_channel(inv)
    root = jnp.sqrt(2.0 * inv) * (1.0 / math.sqrt(L * NP * NZ * M * R))
    slope = res_ref[...] * root
    none = jnp.zeros((G, R), F32)
    rest = jnp.zeros((G, 128 - 2 * R), F32)
    factor_ref[0] = jnp.concatenate([root, slope * inv, rest], axis=1)
    factor_ref[1] = jnp.concatenate([none, -0.5 * slope, rest], axis=1)
    rate = by_group_mode(inv)
    gain = by_group_mode(res_ref[...] * jnp.sqrt(2.0 * inv) * (1.0 / math.sqrt(R)))
    lane = iota((128, 128), 1)
    row = iota((128, 128), 0)
    step = lane.astype(F32)
    head = gain * jnp.exp(-step * rate)
    head_ref[...] = head
    tail_ref[...] = gain * jnp.exp(-(jnp.float32(L) - step) * rate)
    taps = jnp.sum(head.reshape(G, R, L), axis=1)
    skip = jnp.sum(jnp.where(lane == row, skip_ref[...], 0.0), axis=1, keepdims=True)
    for g in range(G):
        c = slice(g * M, (g + 1) * M)
        table = pltpu.roll(jnp.broadcast_to(taps[g : g + 1], (L, L)), 0, 1, stride=1, stride_axis=0)
        table = jnp.where(lane >= row, table, 0.0)
        fwd_ref[c] = dot(product[c], table) + skip[c] * product[c]
        bwd_ref[c] = dot(grad_mixed[c], table, 1, 1) + skip[c] * grad_mixed[c]


def plane_index():
    return lax.axis_index("y") * 4 + lax.axis_index("x")


def to_front(state, quarter):
    return pltpu.roll(state, lax.rem(4 - quarter, 4) * SHARE, 1)


def my_quarter():
    return lax.rem(lax.axis_index("y"), 2) * 2 + lax.rem(lax.axis_index("x"), 2)


def plane_kernel(msg_ref, rate_ref, out_ref, carry_ref):
    rate = rate_ref[...]
    me = plane_index()
    quarter = my_quarter()
    span = jnp.float32(L)
    decay = jnp.exp(-span * rate)
    zero = jnp.zeros((R, CH), F32)
    front_decay = to_front(decay, quarter)
    f, g, f1, h0, h1, own_f = zero, zero, zero, zero, zero, zero
    sums = jnp.zeros((G, 128), F32)
    fronts = []
    for i in range(NP):
        at = plane_slot(i)
        own_f = jnp.where(me == i, f, own_f)
        fwd, bwd = msg_ref[at, :R], to_front(msg_ref[at, R : 2 * R], quarter)
        fwd1, bwd1 = unpack_moments(msg_ref[at, MOMENT_ROW:SUM_ROW])
        fronts.append((bwd, bwd1))
        h0 = h0 + g * bwd
        h1 = h1 + g * bwd1 + f1 * bwd
        f1 = front_decay * (f1 + span * g) + fwd1
        g = front_decay * g + to_front(fwd, quarter)
        f = decay * f + fwd
        sums = sums + msg_ref[at, SUM_ROW:]
    b, e, b1, own_b = zero, zero, zero, zero
    for i in reversed(range(NP)):
        bwd, bwd1 = fronts[i]
        own_b = jnp.where(me == i, b, own_b)
        b1 = front_decay * (b1 + span * e) + bwd1
        e = front_decay * e + bwd
        b = decay * b + msg_ref[plane_slot(i), R : 2 * R]
    carry_ref[:R] = own_f
    carry_ref[R : 2 * R] = own_b
    sums = sums + front_sums(h0, h1, quarter)
    sums = jnp.concatenate([pltpu.roll(sums, 3 * SHARE, 1), pltpu.roll(sums, 2 * SHARE, 1)], axis=0)
    place = iota((R, CH), 1) // SHARE
    rest = jnp.where(place == 1, pltpu.roll(f1, SHARE, 1), jnp.where(place == 2, pltpu.roll(b1, 2 * SHARE, 1), sums))
    z = lax.axis_index("z")
    for i in range(NZ):
        above = z < i
        out_ref[z_slot(i), :R] = jnp.where(above, f, b)
        out_ref[z_slot(i), R:] = jnp.where(place == 0, jnp.where(above, e, g), rest)


def final_kernel(msg_ref, rate_ref, factor_ref, param_ref):
    quarter = my_quarter()
    z = lax.axis_index("z")
    span = jnp.float32(L * NP)
    decay = jnp.exp(-span * to_front(rate_ref[...], quarter))
    zero = jnp.zeros((R, CH), F32)
    f, f1, h0, h1 = zero, zero, zero, zero
    total = zero
    for i in range(NZ):
        at = z_slot(i)
        carry = to_front(msg_ref[at, :R], quarter)
        part = msg_ref[at, R:]
        fwd, bwd = jnp.where(i < z, carry, part), jnp.where(i < z, part, carry)
        bwd1 = pltpu.roll(part, 2 * SHARE, 1)
        h0 = h0 + f * bwd
        h1 = h1 + f * bwd1 + f1 * bwd
        f1 = decay * (f1 + span * f) + pltpu.roll(part, 3 * SHARE, 1)
        f = decay * f + fwd
        total = total + part
    whole = front_sums(h0, h1, quarter) + pltpu.roll(total[:G], SHARE, 1)
    params = whole * factor_ref[0] + pltpu.roll(whole, R, 1) * factor_ref[1]
    group = iota((G, 128), 0) - quarter * (G // 4)
    row = jnp.where(group == 0, params, 0.0)
    for k in range(1, G // 4):
        row = row + jnp.where(group == k, pltpu.roll(params, 2 * R * k, 1), 0.0)
    row = jnp.sum(row, axis=0, keepdims=True)
    for i in range(PEERS):
        param_ref[i] = row


def gather_kernel(part_ref, residue_ref, time_ref):
    rows = part_ref[...].reshape(PEERS, 128)
    columns = jnp.concatenate([rows, jnp.zeros((128 - PEERS, 128), F32)], axis=0).T
    peer = iota((128, 4 * G), 0)
    group = iota((128, 4 * G), 1)
    quarter, core, zh = 3 - peer % 4, peer // 4 % 2, 1 - peer // 8
    first = (zh * 2 + core) * G + quarter * (G // 4)
    out = jnp.zeros((2 * R, 4 * G), F32)
    for k in range(G // 4):
        place = ones_where((group == first + k) & (peer < PEERS)).astype(jnp.bfloat16)
        for part in halves(columns[2 * R * k : 2 * R * (k + 1)]):
            out = out + lax.dot_general(part, place, (((1,), (0,)), ((), ())), preferred_element_type=F32)
    residue_ref[...] = out[:R]
    time_ref[...] = out[R:]


def plane_slot(p):
    return PLANE_ORDER.index(p)


def z_slot(z):
    return jnp.where(lax.axis_index("zh") == 1, Z_ORDER[1].index(z), Z_ORDER[0].index(z))


def plane_groups():
    return [list(PLANE_ORDER)]


def z_groups():
    return [[zh * NZ + z for z in order] for zh, order in enumerate(Z_ORDER)]


def gather_groups():
    groups = []
    index = lambda zh, z, y, x, core: (((zh * NZ + z) * 4 + y) * 4 + x) * 2 + core
    block = [(zh, core, y, x) for zh in (1, 0) for core in (0, 1) for y in (1, 0) for x in (1, 0)]
    for z in range(NZ):
        planes = {0: z, 1: Z_PARTNER[z]}
        for top in (0, 2):
            for left in (0, 2):
                groups.append([index(zh, planes[zh], top + y, left + x, core) for zh, core, y, x in block])
    return groups


def output_kernel(
    q_hbm, k_hbm, v_hbm, ct_hbm, fwd_ref, bwd_ref, head_ref, tail_ref, msg_ref, plane_ref, rate_ref,
    out_ref, gq_ref, gk_ref, gv_ref, skip_ref, q_ref, k_ref, v_ref, ct_ref, sems,
):
    fetch(((q_hbm, q_ref), (k_hbm, k_ref), (v_hbm, v_ref), (ct_hbm, ct_ref)), sems)
    rate = rate_ref[...]
    z = lax.axis_index("z")
    me = plane_index().astype(F32)
    decay = jnp.exp(-jnp.float32(L * NP) * rate)
    own_f = jnp.zeros((R, CH), F32)
    own_b = own_f
    sums = jnp.zeros((G, 128), F32)
    for i in range(NZ):
        own_f = jnp.where(i < z, decay * own_f + msg_ref[z_slot(i), :R], own_f)
        sums = sums + msg_ref[z_slot(i), R + G :]
    for i in reversed(range(NZ)):
        own_b = jnp.where(i > z, decay * own_b + msg_ref[z_slot(i), :R], own_b)
    own_f = plane_ref[:R] + jnp.exp(-(L * me) * rate) * own_f
    own_b = plane_ref[R : 2 * R] + jnp.exp(-(L * (NP - 1 - me)) * rate) * own_b
    lane = iota((128, 128), 1)
    row = iota((128, 128), 0)
    spread = dot(sums, ones_where((row - 3 * SHARE == lane % M) & (row >= 3 * SHARE) & (row < 3 * SHARE + M)))
    spread = jnp.where(iota((G, CH), 1) // M == iota((G, CH), 0), spread, 0.0)
    skip_ref[...] = jnp.sum(spread, axis=0, keepdims=True) * (1.0 / math.sqrt(L * NP * NZ))
    mixed = fwd_ref[...] + dot3(spread_states(own_f), head_ref[...], 0, 0)
    grad_product = bwd_ref[...] + dot3(spread_states(own_b), tail_ref[...], 0, 0)
    out_ref[...] = (v_ref[...].astype(F32) * mixed).astype(jnp.bfloat16)
    gv_ref[...] = (ct_ref[...].astype(F32) * mixed).astype(jnp.bfloat16)
    gq_ref[...] = (grad_product * k_ref[...].astype(F32)).astype(jnp.bfloat16)
    gk_ref[...] = (grad_product * q_ref[...].astype(F32)).astype(jnp.bfloat16)


def shape(*dims, dtype=F32):
    return jax.ShapeDtypeStruct(dims, dtype)


def call(kernel, outs, flops, name, vmem=32 * 1024 * 1024, **options):
    return pl.pallas_call(
        kernel,
        out_shape=outs,
        name=name,
        cost_estimate=pl.CostEstimate(flops=flops, bytes_accessed=500_000, transcendentals=0),
        compiler_params=pltpu.CompilerParams(vmem_limit_bytes=vmem),
        **options,
    )


def per_device(queries, key_inputs, value_inputs, skip_gain, residue, timescale, cotangent):
    arrays = (queries, key_inputs, value_inputs, cotangent)
    hbm = pl.BlockSpec(memory_space=pltpu.HBM)
    local = pl.BlockSpec(memory_space=pltpu.VMEM)
    blocks = [pltpu.VMEM((CH, L), jnp.bfloat16)] * 4
    message = call(
        local_kernel,
        shape(NP, ROWS, 128),
        10**8,
        "local_states",
        vmem=60 * 1024 * 1024,
        in_specs=[hbm] * 5,
        out_specs=hbm,
        scratch_shapes=[
            *blocks,
            pltpu.VMEM((G, R), F32),
            pltpu.VMEM((2 * R, CH), F32),
            pltpu.VMEM((4, 8, CH), F32),
            pltpu.VMEM((G, CH), F32),
            pltpu.SemaphoreType.DMA((5,)),
            pltpu.SemaphoreType.DMA((3 * NP,)),
        ],
    )(*arrays, timescale)
    plane_states = lax.all_to_all(message, ("y", "x"), 0, 0, axis_index_groups=plane_groups())
    *tables, rate, factors = call(
        conv_kernel,
        (*(shape(128, 128),) * 4, shape(R, CH), shape(2, G, 128)),
        10**8,
        "local_conv",
        in_specs=[hbm] * 5 + [local] * 2,
        scratch_shapes=[*blocks, pltpu.VMEM((1, CH), F32), pltpu.SemaphoreType.DMA((5,))],
    )(*arrays, skip_gain.reshape(1, CH), timescale, residue)
    totals, plane_carry = call(plane_kernel, (shape(NZ, Z_ROWS, 128), shape(2 * R, CH)), 10**7, "plane_scan")(
        plane_states, rate
    )
    z_states = lax.all_to_all(totals, ("zh", "z"), 0, 0, axis_index_groups=z_groups())
    params = call(final_kernel, shape(PEERS, 1, 128), 10**7, "z_scan")(z_states, rate, factors)
    params = lax.all_to_all(params, ("zh", "z", "y", "x", "core"), 0, 0, axis_index_groups=gather_groups())
    output, grad_queries, grad_keys, grad_values, grad_skip = call(
        output_kernel,
        (*(shape(CH, L, dtype=jnp.bfloat16),) * 4, shape(1, CH)),
        10**8,
        "outputs",
        in_specs=[hbm] * 4 + [local] * 7,
        scratch_shapes=[*blocks, pltpu.SemaphoreType.DMA((4,))],
    )(*arrays, *tables, z_states, plane_carry, rate)
    grad_residue, grad_time = call(gather_kernel, (shape(R, 4 * G),) * 2, 10**6, "gather")(params)
    return (
        output,
        grad_queries,
        grad_keys,
        grad_values,
        grad_skip.reshape(CH),
        grad_residue.T,
        grad_time.T,
    )


def solution(mesh):
    grid = Mesh(mesh.devices.reshape(NZ, 4, 4, 2, 2), ("z", "y", "x", "zh", "core"))
    seq = ("z", "y", "x")
    ch = ("zh", "core")
    return jax.shard_map(
        per_device,
        mesh=grid,
        in_specs=(P(ch, seq), P(ch, seq), P(ch, seq), P(ch), P(ch, None), P(ch, None), P(ch, seq)),
        out_specs=(P(ch, seq), P(ch, seq), P(ch, seq), P(ch, seq), P(ch), P(), P()),
        check_vma=False,
    )
```

```python
import math

import jax
import jax.numpy as jnp
from jax import lax
from jax.experimental import pallas as pl
from jax.experimental.pallas import tpu as pltpu
from jax.sharding import Mesh, PartitionSpec as P

F32 = jnp.float32
HI = lax.Precision.HIGHEST
L = 128
CH = 128
G = 8
R = 16
M = 16
MOMENT_ROW = 2 * R
SUM_ROW = MOMENT_ROW + R // 2
ROWS = SUM_ROW + G
NP = 16
NZ = 8
SHARE = CH // 4
Z_ROWS = 2 * R
PEERS = 16
PLANE_ORDER = (15, 14, 11, 13, 10, 7, 12, 9, 6, 3, 8, 5, 2, 4, 1, 0)
Z_ORDER = ((7, 0, 6, 1, 5, 2, 4, 3), (3, 4, 2, 5, 1, 6, 0, 7))
Z_PARTNER = (6, 7, 5, 0, 1, 2, 3, 4)
LOWER_FIRST = 7


def dot(a, b, ca=1, cb=0):
    return lax.dot_general(a, b, (((ca,), (cb,)), ((), ())), precision=HI, preferred_element_type=F32)


def halves(value):
    high = value.astype(jnp.bfloat16)
    return high, (value - high.astype(F32)).astype(jnp.bfloat16)


def dot3(a, b, ca=1, cb=0):
    (a_high, a_low), (b_high, b_low) = halves(a), halves(b)
    left = jnp.concatenate([a_high, a_high, a_low], axis=ca)
    right = jnp.concatenate([b_high, b_low, b_high], axis=cb)
    return lax.dot_general(left, right, (((ca,), (cb,)), ((), ())), preferred_element_type=F32)


def pick_dot(pick, b, ca=1, cb=0):
    pick = pick.astype(jnp.bfloat16)
    left = jnp.concatenate([pick, pick], axis=ca)
    right = jnp.concatenate(halves(b), axis=cb)
    return lax.dot_general(left, right, (((ca,), (cb,)), ((), ())), preferred_element_type=F32)


def pick_dot_right(a, pick):
    pick = pick.astype(jnp.bfloat16)
    left = jnp.concatenate(halves(a), axis=1)
    right = jnp.concatenate([pick, pick], axis=0)
    return lax.dot_general(left, right, (((1,), (0,)), ((), ())), preferred_element_type=F32)


def iota(shape, axis):
    return lax.broadcasted_iota(jnp.int32, shape, axis)


def ones_where(cond):
    return jnp.where(cond, jnp.float32(1), jnp.float32(0))


def by_mode_and_channel(table):
    pick = ones_where(iota((G, CH), 1) // M == iota((G, CH), 0))
    return dot(table, pick, 0, 0)


def by_group_mode(table):
    rows = jnp.concatenate([jnp.broadcast_to(table[g : g + 1], (R, R)) for g in range(G)], axis=0)
    rows = jnp.where(iota((G * R, R), 0) % R == iota((G * R, R), 1), rows, 0.0)
    return jnp.sum(rows, axis=1, keepdims=True)


def same_group():
    return iota((128, 128), 0) // M == iota((128, 128), 1) // M


def fold_states(full):
    own = jnp.where(same_group(), full, 0.0)
    return jnp.sum(own.reshape(G, R, CH), axis=0)


def spread_states(state):
    return jnp.where(same_group(), jnp.concatenate([state] * G, axis=0), 0.0)


def front_sums(h0, h1, quarter):
    lane = iota((G, CH), 1)
    pick = ones_where((lane // M + quarter * (SHARE // M) == iota((G, CH), 0)) & (lane < SHARE))
    front = iota((R, CH), 1) < SHARE
    rows = [jnp.where(front, h0, 0.0), jnp.where(front, h1, 0.0), jnp.zeros((CH - 2 * R, CH), F32)]
    return pick_dot(pick, jnp.concatenate(rows, axis=0), 1, 1)


def fetch(pairs, sems):
    copies = [pltpu.make_async_copy(src, dst, sems.at[i]) for i, (src, dst) in enumerate(pairs)]
    for copy in copies:
        copy.start()
    for copy in copies:
        copy.wait()


def quarter_of(y, x):
    return y % 2 * 2 + x % 2


def pack_moments(a, b, quarter):
    packed = jnp.zeros((8, CH), F32)
    for k, piece in enumerate((a[:8], a[8:], b[:8], b[8:])):
        packed = jnp.where(iota((8, CH), 1) // SHARE == k, pltpu.roll(piece, (k - quarter) % 4 * SHARE, 1), packed)
    return packed


def unpack_moments(packed):
    moved = [packed] + [pltpu.roll(packed, CH - k * SHARE, 1) for k in range(1, 4)]
    return jnp.concatenate(moved[:2], axis=0), jnp.concatenate(moved[2:], axis=0)


def local_kernel(
    q_hbm, k_hbm, v_hbm, ct_hbm, tau_hbm, msg_hbm,
    q_ref, k_ref, v_ref, ct_ref, tau_ref, states_ref, packed_ref, sums_ref, sems, out_sems,
):
    pairs = ((tau_hbm, tau_ref), (q_hbm, q_ref), (k_hbm, k_ref), (v_hbm, v_ref), (ct_hbm, ct_ref))
    fetches = [pltpu.make_async_copy(source, target, sems.at[i]) for i, (source, target) in enumerate(pairs)]
    for copy in fetches:
        copy.start()
    fetches[0].wait()
    rate = by_group_mode(1.0 / tau_ref[...])
    lane = iota((128, 128), 1)
    row = iota((128, 128), 0)
    step = lane.astype(F32)
    decay = jnp.exp(-step * rate)
    left = jnp.float32(L) - step
    decay_end = jnp.exp(-left * rate)
    for copy in fetches[1:]:
        copy.wait()
    product = q_ref[...].astype(F32) * k_ref[...].astype(F32)
    grad_mixed = ct_ref[...].astype(F32) * v_ref[...].astype(F32)
    fwd = dot3(jnp.concatenate([decay_end, left * decay_end], axis=0), product, 1, 1)
    bwd = dot3(jnp.concatenate([decay, step * decay], axis=0), grad_mixed, 1, 1)
    states_ref[:R] = fold_states(fwd[:128])
    states_ref[R:] = fold_states(bwd[:128])
    copies = []

    def send(source, i, rows):
        copies.append(pltpu.make_async_copy(source, msg_hbm.at[plane_slot(i), rows], out_sems.at[len(copies)]))
        copies[-1].start()

    for i in range(NP):
        send(states_ref, i, slice(0, MOMENT_ROW))
    moments = (fold_states(fwd[128:]), fold_states(bwd[128:]))
    for quarter in range(4):
        packed_ref[quarter] = pack_moments(*moments, quarter)
    for i in range(NP):
        send(packed_ref.at[quarter_of(i // 4, i % 4)], i, slice(MOMENT_ROW, SUM_ROW))
    flipped = pick_dot_right(product, ones_where(lane + row == L - 1))
    inside = lane + row >= L - 1
    lags = []
    for g in range(G):
        c = slice(g * M, (g + 1) * M)
        outer = jnp.where(inside, dot3(flipped[c], grad_mixed[c], 0, 0), 0.0)
        lags.append(jnp.sum(pltpu.roll(outer, 1, 1, stride=1, stride_axis=0), axis=0, keepdims=True))
    lags = jnp.concatenate(lags, axis=0)
    lags = jnp.concatenate([lags, lags * step[:G]], axis=0)
    modal = dot3(lags, decay, 1, 1)
    modal = jnp.where(iota((2 * G, G * R), 0) % G == iota((2 * G, G * R), 1) // R, modal, 0.0)
    modal = jnp.concatenate([modal[:G], modal[G:]], axis=1)
    fold = iota((2 * G * R, 128), 0)
    fold = ones_where(fold % R + fold // (G * R) * R == iota((2 * G * R, 128), 1))
    skip = jnp.sum(grad_mixed * product, axis=1, keepdims=True)
    skip = jnp.where(row % M == lane - 2 * R, skip, 0.0)
    pick = ones_where(iota((G, CH), 1) // M == iota((G, CH), 0))
    sums_ref[...] = pick_dot_right(modal, fold) + pick_dot(pick, skip)
    for i in range(NP):
        send(sums_ref, i, slice(SUM_ROW, ROWS))
    for copy in copies:
        copy.wait()


def conv_kernel(
    q_hbm, k_hbm, v_hbm, ct_hbm, skip_hbm, tau_ref, res_ref, fwd_ref, bwd_ref, head_ref, tail_ref, rate_ref, factor_ref, q_ref, k_ref, v_ref, ct_ref, skip_ref, sems
):
    fetch(((q_hbm, q_ref), (k_hbm, k_ref), (v_hbm, v_ref), (ct_hbm, ct_ref), (skip_hbm, skip_ref)), sems)
    product = q_ref[...].astype(F32) * k_ref[...].astype(F32)
    grad_mixed = ct_ref[...].astype(F32) * v_ref[...].astype(F32)
    inv = 1.0 / tau_ref[...]
    rate_ref[...] = by_mode_and_channel(inv)
    root = jnp.sqrt(2.0 * inv) * (1.0 / math.sqrt(L * NP * NZ * M * R))
    slope = res_ref[...] * root
    none = jnp.zeros((G, R), F32)
    rest = jnp.zeros((G, 128 - 2 * R), F32)
    factor_ref[0] = jnp.concatenate([root, slope * inv, rest], axis=1)
    factor_ref[1] = jnp.concatenate([none, -0.5 * slope, rest], axis=1)
    rate = by_group_mode(inv)
    gain = by_group_mode(res_ref[...] * jnp.sqrt(2.0 * inv) * (1.0 / math.sqrt(R)))
    lane = iota((128, 128), 1)
    row = iota((128, 128), 0)
    step = lane.astype(F32)
    head = gain * jnp.exp(-step * rate)
    head_ref[...] = head
    tail_ref[...] = gain * jnp.exp(-(jnp.float32(L) - step) * rate)
    taps = jnp.sum(head.reshape(G, R, L), axis=1)
    skip = jnp.sum(jnp.where(lane == row, skip_ref[...], 0.0), axis=1, keepdims=True)
    for g in range(G):
        c = slice(g * M, (g + 1) * M)
        table = pltpu.roll(jnp.broadcast_to(taps[g : g + 1], (L, L)), 0, 1, stride=1, stride_axis=0)
        table = jnp.where(lane >= row, table, 0.0)
        fwd_ref[c] = dot(product[c], table) + skip[c] * product[c]
        bwd_ref[c] = dot(grad_mixed[c], table, 1, 1) + skip[c] * grad_mixed[c]


def plane_index():
    return lax.axis_index("y") * 4 + lax.axis_index("x")


def to_front(state, quarter):
    return pltpu.roll(state, lax.rem(4 - quarter, 4) * SHARE, 1)


def my_quarter():
    return lax.rem(lax.axis_index("y"), 2) * 2 + lax.rem(lax.axis_index("x"), 2)


def plane_kernel(msg_ref, rate_ref, out_ref, carry_ref):
    rate = rate_ref[...]
    me = plane_index()
    quarter = my_quarter()
    span = jnp.float32(L)
    decay = jnp.exp(-span * rate)
    zero = jnp.zeros((R, CH), F32)
    front_decay = to_front(decay, quarter)
    f, g, f1, h0, h1, own_f = zero, zero, zero, zero, zero, zero
    sums = jnp.zeros((G, 128), F32)
    fronts = []
    for i in range(NP):
        at = plane_slot(i)
        own_f = jnp.where(me == i, f, own_f)
        fwd, bwd = msg_ref[at, :R], to_front(msg_ref[at, R : 2 * R], quarter)
        fwd1, bwd1 = unpack_moments(msg_ref[at, MOMENT_ROW:SUM_ROW])
        fronts.append((bwd, bwd1))
        h0 = h0 + g * bwd
        h1 = h1 + g * bwd1 + f1 * bwd
        f1 = front_decay * (f1 + span * g) + fwd1
        g = front_decay * g + to_front(fwd, quarter)
        f = decay * f + fwd
        sums = sums + msg_ref[at, SUM_ROW:]
    b, e, b1, own_b = zero, zero, zero, zero
    for i in reversed(range(NP)):
        bwd, bwd1 = fronts[i]
        own_b = jnp.where(me == i, b, own_b)
        b1 = front_decay * (b1 + span * e) + bwd1
        e = front_decay * e + bwd
        b = decay * b + msg_ref[plane_slot(i), R : 2 * R]
    carry_ref[:R] = own_f
    carry_ref[R : 2 * R] = own_b
    sums = sums + front_sums(h0, h1, quarter)
    sums = jnp.concatenate([pltpu.roll(sums, 3 * SHARE, 1), pltpu.roll(sums, 2 * SHARE, 1)], axis=0)
    place = iota((R, CH), 1) // SHARE
    rest = jnp.where(place == 1, pltpu.roll(f1, SHARE, 1), jnp.where(place == 2, pltpu.roll(b1, 2 * SHARE, 1), sums))
    z = lax.axis_index("z")
    for i in range(NZ):
        above = z < i
        out_ref[z_slot(i), :R] = jnp.where(above, f, b)
        out_ref[z_slot(i), R:] = jnp.where(place == 0, jnp.where(above, e, g), rest)


def final_kernel(msg_ref, rate_ref, factor_ref, param_ref):
    quarter = my_quarter()
    z = lax.axis_index("z")
    span = jnp.float32(L * NP)
    decay = jnp.exp(-span * to_front(rate_ref[...], quarter))
    zero = jnp.zeros((R, CH), F32)
    f, f1, h0, h1 = zero, zero, zero, zero
    total = zero
    for i in range(NZ):
        at = z_slot(i)
        carry = to_front(msg_ref[at, :R], quarter)
        part = msg_ref[at, R:]
        fwd, bwd = jnp.where(i < z, carry, part), jnp.where(i < z, part, carry)
        bwd1 = pltpu.roll(part, 2 * SHARE, 1)
        h0 = h0 + f * bwd
        h1 = h1 + f * bwd1 + f1 * bwd
        f1 = decay * (f1 + span * f) + pltpu.roll(part, 3 * SHARE, 1)
        f = decay * f + fwd
        total = total + part
    whole = front_sums(h0, h1, quarter) + pltpu.roll(total[:G], SHARE, 1)
    params = whole * factor_ref[0] + pltpu.roll(whole, R, 1) * factor_ref[1]
    group = iota((G, 128), 0) - quarter * (G // 4)
    row = jnp.where(group == 0, params, 0.0)
    for k in range(1, G // 4):
        row = row + jnp.where(group == k, pltpu.roll(params, 2 * R * k, 1), 0.0)
    row = jnp.sum(row, axis=0, keepdims=True)
    for i in range(PEERS):
        param_ref[i] = row


def gather_kernel(part_ref, residue_ref, time_ref):
    rows = part_ref[...].reshape(PEERS, 128)
    columns = jnp.concatenate([rows, jnp.zeros((128 - PEERS, 128), F32)], axis=0).T
    peer = iota((128, 4 * G), 0)
    group = iota((128, 4 * G), 1)
    lower = jnp.where(lax.axis_index("zh") == 1, Z_PARTNER[LOWER_FIRST], LOWER_FIRST)
    lower_first = jnp.where(lax.axis_index("z") == lower, 1, 0)
    quarter, core = 3 - peer % 4, peer // 4 % 2
    zh = lower_first + (1 - 2 * lower_first) * (1 - peer // 8)
    first = (zh * 2 + core) * G + quarter * (G // 4)
    out = jnp.zeros((2 * R, 4 * G), F32)
    for k in range(G // 4):
        place = ones_where((group == first + k) & (peer < PEERS)).astype(jnp.bfloat16)
        for part in halves(columns[2 * R * k : 2 * R * (k + 1)]):
            out = out + lax.dot_general(part, place, (((1,), (0,)), ((), ())), preferred_element_type=F32)
    residue_ref[...] = out[:R]
    time_ref[...] = out[R:]


def plane_slot(p):
    return PLANE_ORDER.index(p)


def z_slot(z):
    return jnp.where(lax.axis_index("zh") == 1, Z_ORDER[1].index(z), Z_ORDER[0].index(z))


def plane_groups():
    return [list(PLANE_ORDER)]


def z_groups():
    return [[zh * NZ + z for z in order] for zh, order in enumerate(Z_ORDER)]


def gather_groups():
    groups = []
    index = lambda zh, z, y, x, core: (((zh * NZ + z) * 4 + y) * 4 + x) * 2 + core
    block = [(core, y, x) for core in (0, 1) for y in (1, 0) for x in (1, 0)]
    for z in range(NZ):
        planes = {0: z, 1: Z_PARTNER[z]}
        for top in (0, 2):
            for left in (0, 2):
                order = (0, 1) if z == LOWER_FIRST else (1, 0)
                groups.append([index(zh, planes[zh], top + y, left + x, core) for zh in order for core, y, x in block])
    return groups


def output_kernel(
    q_hbm, k_hbm, v_hbm, ct_hbm, fwd_ref, bwd_ref, head_ref, tail_ref, msg_ref, plane_ref, rate_ref,
    out_ref, gq_ref, gk_ref, gv_ref, skip_ref, q_ref, k_ref, v_ref, ct_ref, sems,
):
    fetch(((q_hbm, q_ref), (k_hbm, k_ref), (v_hbm, v_ref), (ct_hbm, ct_ref)), sems)
    rate = rate_ref[...]
    z = lax.axis_index("z")
    me = plane_index().astype(F32)
    decay = jnp.exp(-jnp.float32(L * NP) * rate)
    own_f = jnp.zeros((R, CH), F32)
    own_b = own_f
    sums = jnp.zeros((G, 128), F32)
    for i in range(NZ):
        own_f = jnp.where(i < z, decay * own_f + msg_ref[z_slot(i), :R], own_f)
        sums = sums + msg_ref[z_slot(i), R + G :]
    for i in reversed(range(NZ)):
        own_b = jnp.where(i > z, decay * own_b + msg_ref[z_slot(i), :R], own_b)
    own_f = plane_ref[:R] + jnp.exp(-(L * me) * rate) * own_f
    own_b = plane_ref[R : 2 * R] + jnp.exp(-(L * (NP - 1 - me)) * rate) * own_b
    lane = iota((128, 128), 1)
    row = iota((128, 128), 0)
    spread = dot(sums, ones_where((row - 3 * SHARE == lane % M) & (row >= 3 * SHARE) & (row < 3 * SHARE + M)))
    spread = jnp.where(iota((G, CH), 1) // M == iota((G, CH), 0), spread, 0.0)
    skip_ref[...] = jnp.sum(spread, axis=0, keepdims=True) * (1.0 / math.sqrt(L * NP * NZ))
    mixed = fwd_ref[...] + dot3(spread_states(own_f), head_ref[...], 0, 0)
    grad_product = bwd_ref[...] + dot3(spread_states(own_b), tail_ref[...], 0, 0)
    out_ref[...] = (v_ref[...].astype(F32) * mixed).astype(jnp.bfloat16)
    gv_ref[...] = (ct_ref[...].astype(F32) * mixed).astype(jnp.bfloat16)
    gq_ref[...] = (grad_product * k_ref[...].astype(F32)).astype(jnp.bfloat16)
    gk_ref[...] = (grad_product * q_ref[...].astype(F32)).astype(jnp.bfloat16)


def shape(*dims, dtype=F32):
    return jax.ShapeDtypeStruct(dims, dtype)


def call(kernel, outs, flops, name, vmem=32 * 1024 * 1024, **options):
    return pl.pallas_call(
        kernel,
        out_shape=outs,
        name=name,
        cost_estimate=pl.CostEstimate(flops=flops, bytes_accessed=500_000, transcendentals=0),
        compiler_params=pltpu.CompilerParams(vmem_limit_bytes=vmem),
        **options,
    )


def per_device(queries, key_inputs, value_inputs, skip_gain, residue, timescale, cotangent):
    arrays = (queries, key_inputs, value_inputs, cotangent)
    hbm = pl.BlockSpec(memory_space=pltpu.HBM)
    local = pl.BlockSpec(memory_space=pltpu.VMEM)
    blocks = [pltpu.VMEM((CH, L), jnp.bfloat16)] * 4
    message = call(
        local_kernel,
        shape(NP, ROWS, 128),
        10**8,
        "local_states",
        vmem=60 * 1024 * 1024,
        in_specs=[hbm] * 5,
        out_specs=hbm,
        scratch_shapes=[
            *blocks,
            pltpu.VMEM((G, R), F32),
            pltpu.VMEM((2 * R, CH), F32),
            pltpu.VMEM((4, 8, CH), F32),
            pltpu.VMEM((G, CH), F32),
            pltpu.SemaphoreType.DMA((5,)),
            pltpu.SemaphoreType.DMA((3 * NP,)),
        ],
    )(*arrays, timescale)
    plane_states = lax.all_to_all(message, ("y", "x"), 0, 0, axis_index_groups=plane_groups())
    *tables, rate, factors = call(
        conv_kernel,
        (*(shape(128, 128),) * 4, shape(R, CH), shape(2, G, 128)),
        10**8,
        "local_conv",
        in_specs=[hbm] * 5 + [local] * 2,
        scratch_shapes=[*blocks, pltpu.VMEM((1, CH), F32), pltpu.SemaphoreType.DMA((5,))],
    )(*arrays, skip_gain.reshape(1, CH), timescale, residue)
    totals, plane_carry = call(plane_kernel, (shape(NZ, Z_ROWS, 128), shape(2 * R, CH)), 10**7, "plane_scan")(
        plane_states, rate
    )
    z_states = lax.all_to_all(totals, ("zh", "z"), 0, 0, axis_index_groups=z_groups())
    params = call(final_kernel, shape(PEERS, 1, 128), 10**7, "z_scan")(z_states, rate, factors)
    params = lax.all_to_all(params, ("zh", "z", "y", "x", "core"), 0, 0, axis_index_groups=gather_groups())
    output, grad_queries, grad_keys, grad_values, grad_skip = call(
        output_kernel,
        (*(shape(CH, L, dtype=jnp.bfloat16),) * 4, shape(1, CH)),
        10**8,
        "outputs",
        in_specs=[hbm] * 4 + [local] * 7,
        scratch_shapes=[*blocks, pltpu.SemaphoreType.DMA((4,))],
    )(*arrays, *tables, z_states, plane_carry, rate)
    grad_residue, grad_time = call(gather_kernel, (shape(R, 4 * G),) * 2, 10**6, "gather")(params)
    return (
        output,
        grad_queries,
        grad_keys,
        grad_values,
        grad_skip.reshape(CH),
        grad_residue.T,
        grad_time.T,
    )


def solution(mesh):
    grid = Mesh(mesh.devices.reshape(NZ, 4, 4, 2, 2), ("z", "y", "x", "zh", "core"))
    seq = ("z", "y", "x")
    ch = ("zh", "core")
    return jax.shard_map(
        per_device,
        mesh=grid,
        in_specs=(P(ch, seq), P(ch, seq), P(ch, seq), P(ch), P(ch, None), P(ch, None), P(ch, seq)),
        out_specs=(P(ch, seq), P(ch, seq), P(ch, seq), P(ch, seq), P(ch), P(), P()),
        check_vma=False,
    )
```

```python
import math

import jax
import jax.numpy as jnp
from jax import lax
from jax.experimental import pallas as pl
from jax.experimental.pallas import tpu as pltpu
from jax.sharding import Mesh, PartitionSpec as P

F32 = jnp.float32
HI = lax.Precision.HIGHEST
L = 128
CH = 128
G = 8
R = 16
M = 16
MOMENT_ROW = 2 * R
SUM_ROW = MOMENT_ROW + R // 2
ROWS = SUM_ROW + G
NP = 16
NZ = 8
SHARE = CH // 4
Z_ROWS = 2 * R
PEERS = 16
PLANE_ORDER = (15, 14, 11, 13, 10, 7, 12, 9, 6, 3, 8, 5, 2, 4, 1, 0)
Z_ORDER = ((7, 0, 6, 1, 5, 2, 4, 3), (3, 4, 2, 5, 1, 6, 0, 7))
Z_PARTNER = (6, 5, 4, 7, 0, 1, 2, 3)


def dot(a, b, ca=1, cb=0):
    return lax.dot_general(a, b, (((ca,), (cb,)), ((), ())), precision=HI, preferred_element_type=F32)


def halves(value):
    high = value.astype(jnp.bfloat16)
    return high, (value - high.astype(F32)).astype(jnp.bfloat16)


def dot3(a, b, ca=1, cb=0):
    (a_high, a_low), (b_high, b_low) = halves(a), halves(b)
    left = jnp.concatenate([a_high, a_high, a_low], axis=ca)
    right = jnp.concatenate([b_high, b_low, b_high], axis=cb)
    return lax.dot_general(left, right, (((ca,), (cb,)), ((), ())), preferred_element_type=F32)


def pick_dot(pick, b, ca=1, cb=0):
    pick = pick.astype(jnp.bfloat16)
    left = jnp.concatenate([pick, pick], axis=ca)
    right = jnp.concatenate(halves(b), axis=cb)
    return lax.dot_general(left, right, (((ca,), (cb,)), ((), ())), preferred_element_type=F32)


def pick_dot_right(a, pick):
    pick = pick.astype(jnp.bfloat16)
    left = jnp.concatenate(halves(a), axis=1)
    right = jnp.concatenate([pick, pick], axis=0)
    return lax.dot_general(left, right, (((1,), (0,)), ((), ())), preferred_element_type=F32)


def iota(shape, axis):
    return lax.broadcasted_iota(jnp.int32, shape, axis)


def ones_where(cond):
    return jnp.where(cond, jnp.float32(1), jnp.float32(0))


def by_mode_and_channel(table):
    pick = ones_where(iota((G, CH), 1) // M == iota((G, CH), 0))
    return dot(table, pick, 0, 0)


def by_group_mode(table):
    rows = jnp.concatenate([jnp.broadcast_to(table[g : g + 1], (R, R)) for g in range(G)], axis=0)
    rows = jnp.where(iota((G * R, R), 0) % R == iota((G * R, R), 1), rows, 0.0)
    return jnp.sum(rows, axis=1, keepdims=True)


def same_group():
    return iota((128, 128), 0) // M == iota((128, 128), 1) // M


def fold_states(full):
    own = jnp.where(same_group(), full, 0.0)
    return jnp.sum(own.reshape(G, R, CH), axis=0)


def spread_states(state):
    return jnp.where(same_group(), jnp.concatenate([state] * G, axis=0), 0.0)


def front_sums(h0, h1, quarter):
    lane = iota((G, CH), 1)
    pick = ones_where((lane // M + quarter * (SHARE // M) == iota((G, CH), 0)) & (lane < SHARE))
    front = iota((R, CH), 1) < SHARE
    rows = [jnp.where(front, h0, 0.0), jnp.where(front, h1, 0.0), jnp.zeros((CH - 2 * R, CH), F32)]
    return pick_dot(pick, jnp.concatenate(rows, axis=0), 1, 1)


def fetch(pairs, sems):
    copies = [pltpu.make_async_copy(src, dst, sems.at[i]) for i, (src, dst) in enumerate(pairs)]
    for copy in copies:
        copy.start()
    for copy in copies:
        copy.wait()


def quarter_of(y, x):
    return y % 2 * 2 + x % 2


def pack_moments(a, b, quarter):
    packed = jnp.zeros((8, CH), F32)
    for k, piece in enumerate((a[:8], a[8:], b[:8], b[8:])):
        packed = jnp.where(iota((8, CH), 1) // SHARE == k, pltpu.roll(piece, (k - quarter) % 4 * SHARE, 1), packed)
    return packed


def unpack_moments(packed):
    moved = [packed] + [pltpu.roll(packed, CH - k * SHARE, 1) for k in range(1, 4)]
    return jnp.concatenate(moved[:2], axis=0), jnp.concatenate(moved[2:], axis=0)


def local_kernel(
    q_hbm, k_hbm, v_hbm, ct_hbm, tau_hbm, msg_hbm,
    q_ref, k_ref, v_ref, ct_ref, tau_ref, states_ref, packed_ref, sums_ref, sems, out_sems,
):
    pairs = ((tau_hbm, tau_ref), (q_hbm, q_ref), (k_hbm, k_ref), (v_hbm, v_ref), (ct_hbm, ct_ref))
    fetches = [pltpu.make_async_copy(source, target, sems.at[i]) for i, (source, target) in enumerate(pairs)]
    for copy in fetches:
        copy.start()
    fetches[0].wait()
    rate = by_group_mode(1.0 / tau_ref[...])
    lane = iota((128, 128), 1)
    row = iota((128, 128), 0)
    step = lane.astype(F32)
    decay = jnp.exp(-step * rate)
    left = jnp.float32(L) - step
    decay_end = jnp.exp(-left * rate)
    for copy in fetches[1:]:
        copy.wait()
    product = q_ref[...].astype(F32) * k_ref[...].astype(F32)
    grad_mixed = ct_ref[...].astype(F32) * v_ref[...].astype(F32)
    fwd = dot3(jnp.concatenate([decay_end, left * decay_end], axis=0), product, 1, 1)
    bwd = dot3(jnp.concatenate([decay, step * decay], axis=0), grad_mixed, 1, 1)
    states_ref[:R] = fold_states(fwd[:128])
    states_ref[R:] = fold_states(bwd[:128])
    copies = []

    def send(source, i, rows):
        copies.append(pltpu.make_async_copy(source, msg_hbm.at[plane_slot(i), rows], out_sems.at[len(copies)]))
        copies[-1].start()

    for i in range(NP):
        send(states_ref, i, slice(0, MOMENT_ROW))
    moments = (fold_states(fwd[128:]), fold_states(bwd[128:]))
    for quarter in range(4):
        packed_ref[quarter] = pack_moments(*moments, quarter)
    for i in range(NP):
        send(packed_ref.at[quarter_of(i // 4, i % 4)], i, slice(MOMENT_ROW, SUM_ROW))
    flipped = pick_dot_right(product, ones_where(lane + row == L - 1))
    inside = lane + row >= L - 1
    lags = []
    for g in range(G):
        c = slice(g * M, (g + 1) * M)
        outer = jnp.where(inside, dot3(flipped[c], grad_mixed[c], 0, 0), 0.0)
        lags.append(jnp.sum(pltpu.roll(outer, 1, 1, stride=1, stride_axis=0), axis=0, keepdims=True))
    lags = jnp.concatenate(lags, axis=0)
    lags = jnp.concatenate([lags, lags * step[:G]], axis=0)
    modal = dot3(lags, decay, 1, 1)
    modal = jnp.where(iota((2 * G, G * R), 0) % G == iota((2 * G, G * R), 1) // R, modal, 0.0)
    modal = jnp.concatenate([modal[:G], modal[G:]], axis=1)
    fold = iota((2 * G * R, 128), 0)
    fold = ones_where(fold % R + fold // (G * R) * R == iota((2 * G * R, 128), 1))
    skip = jnp.sum(grad_mixed * product, axis=1, keepdims=True)
    skip = jnp.where(row % M == lane - 2 * R, skip, 0.0)
    pick = ones_where(iota((G, CH), 1) // M == iota((G, CH), 0))
    sums_ref[...] = pick_dot_right(modal, fold) + pick_dot(pick, skip)
    for i in range(NP):
        send(sums_ref, i, slice(SUM_ROW, ROWS))
    for copy in copies:
        copy.wait()


def conv_kernel(
    q_hbm, k_hbm, v_hbm, ct_hbm, skip_hbm, tau_ref, res_ref, fwd_ref, bwd_ref, head_ref, tail_ref, rate_ref, factor_ref, q_ref, k_ref, v_ref, ct_ref, skip_ref, sems
):
    fetch(((q_hbm, q_ref), (k_hbm, k_ref), (v_hbm, v_ref), (ct_hbm, ct_ref), (skip_hbm, skip_ref)), sems)
    product = q_ref[...].astype(F32) * k_ref[...].astype(F32)
    grad_mixed = ct_ref[...].astype(F32) * v_ref[...].astype(F32)
    inv = 1.0 / tau_ref[...]
    rate_ref[...] = by_mode_and_channel(inv)
    root = jnp.sqrt(2.0 * inv) * (1.0 / math.sqrt(L * NP * NZ * M * R))
    slope = res_ref[...] * root
    none = jnp.zeros((G, R), F32)
    rest = jnp.zeros((G, 128 - 2 * R), F32)
    factor_ref[0] = jnp.concatenate([root, slope * inv, rest], axis=1)
    factor_ref[1] = jnp.concatenate([none, -0.5 * slope, rest], axis=1)
    rate = by_group_mode(inv)
    gain = by_group_mode(res_ref[...] * jnp.sqrt(2.0 * inv) * (1.0 / math.sqrt(R)))
    lane = iota((128, 128), 1)
    row = iota((128, 128), 0)
    step = lane.astype(F32)
    head = gain * jnp.exp(-step * rate)
    head_ref[...] = head
    tail_ref[...] = gain * jnp.exp(-(jnp.float32(L) - step) * rate)
    taps = jnp.sum(head.reshape(G, R, L), axis=1)
    skip = jnp.sum(jnp.where(lane == row, skip_ref[...], 0.0), axis=1, keepdims=True)
    for g in range(G):
        c = slice(g * M, (g + 1) * M)
        table = pltpu.roll(jnp.broadcast_to(taps[g : g + 1], (L, L)), 0, 1, stride=1, stride_axis=0)
        table = jnp.where(lane >= row, table, 0.0)
        fwd_ref[c] = dot(product[c], table) + skip[c] * product[c]
        bwd_ref[c] = dot(grad_mixed[c], table, 1, 1) + skip[c] * grad_mixed[c]


def plane_index():
    return lax.axis_index("y") * 4 + lax.axis_index("x")


def to_front(state, quarter):
    return pltpu.roll(state, lax.rem(4 - quarter, 4) * SHARE, 1)


def my_quarter():
    return lax.rem(lax.axis_index("y"), 2) * 2 + lax.rem(lax.axis_index("x"), 2)


def plane_kernel(msg_ref, rate_ref, out_ref, carry_ref):
    rate = rate_ref[...]
    me = plane_index()
    quarter = my_quarter()
    span = jnp.float32(L)
    decay = jnp.exp(-span * rate)
    zero = jnp.zeros((R, CH), F32)
    front_decay = to_front(decay, quarter)
    f, g, f1, h0, h1, own_f = zero, zero, zero, zero, zero, zero
    sums = jnp.zeros((G, 128), F32)
    fronts = []
    for i in range(NP):
        at = plane_slot(i)
        own_f = jnp.where(me == i, f, own_f)
        fwd, bwd = msg_ref[at, :R], to_front(msg_ref[at, R : 2 * R], quarter)
        fwd1, bwd1 = unpack_moments(msg_ref[at, MOMENT_ROW:SUM_ROW])
        fronts.append((bwd, bwd1))
        h0 = h0 + g * bwd
        h1 = h1 + g * bwd1 + f1 * bwd
        f1 = front_decay * (f1 + span * g) + fwd1
        g = front_decay * g + to_front(fwd, quarter)
        f = decay * f + fwd
        sums = sums + msg_ref[at, SUM_ROW:]
    b, e, b1, own_b = zero, zero, zero, zero
    for i in reversed(range(NP)):
        bwd, bwd1 = fronts[i]
        own_b = jnp.where(me == i, b, own_b)
        b1 = front_decay * (b1 + span * e) + bwd1
        e = front_decay * e + bwd
        b = decay * b + msg_ref[plane_slot(i), R : 2 * R]
    carry_ref[:R] = own_f
    carry_ref[R : 2 * R] = own_b
    sums = sums + front_sums(h0, h1, quarter)
    sums = jnp.concatenate([pltpu.roll(sums, 3 * SHARE, 1), pltpu.roll(sums, 2 * SHARE, 1)], axis=0)
    place = iota((R, CH), 1) // SHARE
    rest = jnp.where(place == 1, pltpu.roll(f1, SHARE, 1), jnp.where(place == 2, pltpu.roll(b1, 2 * SHARE, 1), sums))
    z = lax.axis_index("z")
    for i in range(NZ):
        above = z < i
        out_ref[z_slot(i), :R] = jnp.where(above, f, b)
        out_ref[z_slot(i), R:] = jnp.where(place == 0, jnp.where(above, e, g), rest)


def final_kernel(msg_ref, rate_ref, factor_ref, param_ref):
    quarter = my_quarter()
    z = lax.axis_index("z")
    span = jnp.float32(L * NP)
    decay = jnp.exp(-span * to_front(rate_ref[...], quarter))
    zero = jnp.zeros((R, CH), F32)
    f, f1, h0, h1 = zero, zero, zero, zero
    total = zero
    for i in range(NZ):
        at = z_slot(i)
        carry = to_front(msg_ref[at, :R], quarter)
        part = msg_ref[at, R:]
        fwd, bwd = jnp.where(i < z, carry, part), jnp.where(i < z, part, carry)
        bwd1 = pltpu.roll(part, 2 * SHARE, 1)
        h0 = h0 + f * bwd
        h1 = h1 + f * bwd1 + f1 * bwd
        f1 = decay * (f1 + span * f) + pltpu.roll(part, 3 * SHARE, 1)
        f = decay * f + fwd
        total = total + part
    whole = front_sums(h0, h1, quarter) + pltpu.roll(total[:G], SHARE, 1)
    params = whole * factor_ref[0] + pltpu.roll(whole, R, 1) * factor_ref[1]
    group = iota((G, 128), 0) - quarter * (G // 4)
    row = jnp.where(group == 0, params, 0.0)
    for k in range(1, G // 4):
        row = row + jnp.where(group == k, pltpu.roll(params, 2 * R * k, 1), 0.0)
    row = jnp.sum(row, axis=0, keepdims=True)
    for i in range(PEERS):
        param_ref[i] = row


def gather_kernel(part_ref, residue_ref, time_ref):
    rows = part_ref[...].reshape(PEERS, 128)
    columns = jnp.concatenate([rows, jnp.zeros((128 - PEERS, 128), F32)], axis=0).T
    peer = iota((128, 4 * G), 0)
    group = iota((128, 4 * G), 1)
    quarter, core, zh = 3 - peer % 4, peer // 4 % 2, 1 - peer // 8
    first = (zh * 2 + core) * G + quarter * (G // 4)
    out = jnp.zeros((2 * R, 4 * G), F32)
    for k in range(G // 4):
        place = ones_where((group == first + k) & (peer < PEERS)).astype(jnp.bfloat16)
        for part in halves(columns[2 * R * k : 2 * R * (k + 1)]):
            out = out + lax.dot_general(part, place, (((1,), (0,)), ((), ())), preferred_element_type=F32)
    residue_ref[...] = out[:R]
    time_ref[...] = out[R:]


def plane_slot(p):
    return PLANE_ORDER.index(p)


def z_slot(z):
    return jnp.where(lax.axis_index("zh") == 1, Z_ORDER[1].index(z), Z_ORDER[0].index(z))


def plane_groups():
    return [list(PLANE_ORDER)]


def z_groups():
    return [[zh * NZ + z for z in order] for zh, order in enumerate(Z_ORDER)]


def gather_groups():
    groups = []
    index = lambda zh, z, y, x, core: (((zh * NZ + z) * 4 + y) * 4 + x) * 2 + core
    block = [(zh, core, y, x) for zh in (1, 0) for core in (0, 1) for y in (1, 0) for x in (1, 0)]
    for z in range(NZ):
        planes = {0: z, 1: Z_PARTNER[z]}
        for top in (0, 2):
            for left in (0, 2):
                groups.append([index(zh, planes[zh], top + y, left + x, core) for zh, core, y, x in block])
    return groups


def output_kernel(
    q_hbm, k_hbm, v_hbm, ct_hbm, fwd_ref, bwd_ref, head_ref, tail_ref, msg_ref, plane_ref, rate_ref,
    out_ref, gq_ref, gk_ref, gv_ref, skip_ref, q_ref, k_ref, v_ref, ct_ref, sems,
):
    fetch(((q_hbm, q_ref), (k_hbm, k_ref), (v_hbm, v_ref), (ct_hbm, ct_ref)), sems)
    rate = rate_ref[...]
    z = lax.axis_index("z")
    me = plane_index().astype(F32)
    decay = jnp.exp(-jnp.float32(L * NP) * rate)
    own_f = jnp.zeros((R, CH), F32)
    own_b = own_f
    sums = jnp.zeros((G, 128), F32)
    for i in range(NZ):
        own_f = jnp.where(i < z, decay * own_f + msg_ref[z_slot(i), :R], own_f)
        sums = sums + msg_ref[z_slot(i), R + G :]
    for i in reversed(range(NZ)):
        own_b = jnp.where(i > z, decay * own_b + msg_ref[z_slot(i), :R], own_b)
    own_f = plane_ref[:R] + jnp.exp(-(L * me) * rate) * own_f
    own_b = plane_ref[R : 2 * R] + jnp.exp(-(L * (NP - 1 - me)) * rate) * own_b
    lane = iota((128, 128), 1)
    row = iota((128, 128), 0)
    spread = dot(sums, ones_where((row - 3 * SHARE == lane % M) & (row >= 3 * SHARE) & (row < 3 * SHARE + M)))
    spread = jnp.where(iota((G, CH), 1) // M == iota((G, CH), 0), spread, 0.0)
    skip_ref[...] = jnp.sum(spread, axis=0, keepdims=True) * (1.0 / math.sqrt(L * NP * NZ))
    mixed = fwd_ref[...] + dot3(spread_states(own_f), head_ref[...], 0, 0)
    grad_product = bwd_ref[...] + dot3(spread_states(own_b), tail_ref[...], 0, 0)
    out_ref[...] = (v_ref[...].astype(F32) * mixed).astype(jnp.bfloat16)
    gv_ref[...] = (ct_ref[...].astype(F32) * mixed).astype(jnp.bfloat16)
    gq_ref[...] = (grad_product * k_ref[...].astype(F32)).astype(jnp.bfloat16)
    gk_ref[...] = (grad_product * q_ref[...].astype(F32)).astype(jnp.bfloat16)


def shape(*dims, dtype=F32):
    return jax.ShapeDtypeStruct(dims, dtype)


def call(kernel, outs, flops, name, vmem=32 * 1024 * 1024, **options):
    return pl.pallas_call(
        kernel,
        out_shape=outs,
        name=name,
        cost_estimate=pl.CostEstimate(flops=flops, bytes_accessed=500_000, transcendentals=0),
        compiler_params=pltpu.CompilerParams(vmem_limit_bytes=vmem),
        **options,
    )


def per_device(queries, key_inputs, value_inputs, skip_gain, residue, timescale, cotangent):
    arrays = (queries, key_inputs, value_inputs, cotangent)
    hbm = pl.BlockSpec(memory_space=pltpu.HBM)
    local = pl.BlockSpec(memory_space=pltpu.VMEM)
    blocks = [pltpu.VMEM((CH, L), jnp.bfloat16)] * 4
    message = call(
        local_kernel,
        shape(NP, ROWS, 128),
        10**8,
        "local_states",
        vmem=60 * 1024 * 1024,
        in_specs=[hbm] * 5,
        out_specs=hbm,
        scratch_shapes=[
            *blocks,
            pltpu.VMEM((G, R), F32),
            pltpu.VMEM((2 * R, CH), F32),
            pltpu.VMEM((4, 8, CH), F32),
            pltpu.VMEM((G, CH), F32),
            pltpu.SemaphoreType.DMA((5,)),
            pltpu.SemaphoreType.DMA((3 * NP,)),
        ],
    )(*arrays, timescale)
    plane_states = lax.all_to_all(message, ("y", "x"), 0, 0, axis_index_groups=plane_groups())
    *tables, rate, factors = call(
        conv_kernel,
        (*(shape(128, 128),) * 4, shape(R, CH), shape(2, G, 128)),
        10**8,
        "local_conv",
        in_specs=[hbm] * 5 + [local] * 2,
        scratch_shapes=[*blocks, pltpu.VMEM((1, CH), F32), pltpu.SemaphoreType.DMA((5,))],
    )(*arrays, skip_gain.reshape(1, CH), timescale, residue)
    totals, plane_carry = call(plane_kernel, (shape(NZ, Z_ROWS, 128), shape(2 * R, CH)), 10**7, "plane_scan")(
        plane_states, rate
    )
    z_states = lax.all_to_all(totals, ("zh", "z"), 0, 0, axis_index_groups=z_groups())
    params = call(final_kernel, shape(PEERS, 1, 128), 10**7, "z_scan")(z_states, rate, factors)
    params = lax.all_to_all(params, ("zh", "z", "y", "x", "core"), 0, 0, axis_index_groups=gather_groups())
    output, grad_queries, grad_keys, grad_values, grad_skip = call(
        output_kernel,
        (*(shape(CH, L, dtype=jnp.bfloat16),) * 4, shape(1, CH)),
        10**8,
        "outputs",
        in_specs=[hbm] * 4 + [local] * 7,
        scratch_shapes=[*blocks, pltpu.SemaphoreType.DMA((4,))],
    )(*arrays, *tables, z_states, plane_carry, rate)
    grad_residue, grad_time = call(gather_kernel, (shape(R, 4 * G),) * 2, 10**6, "gather")(params)
    return (
        output,
        grad_queries,
        grad_keys,
        grad_values,
        grad_skip.reshape(CH),
        grad_residue.T,
        grad_time.T,
    )


def solution(mesh):
    grid = Mesh(mesh.devices.reshape(NZ, 4, 4, 2, 2), ("z", "y", "x", "zh", "core"))
    seq = ("z", "y", "x")
    ch = ("zh", "core")
    return jax.shard_map(
        per_device,
        mesh=grid,
        in_specs=(P(ch, seq), P(ch, seq), P(ch, seq), P(ch), P(ch, None), P(ch, None), P(ch, seq)),
        out_specs=(P(ch, seq), P(ch, seq), P(ch, seq), P(ch, seq), P(ch), P(), P()),
        check_vma=False,
    )
```
